32 devices in a mesh: mod: 2 (over core), seq: 4 (over z), tp: 4 (over y, x).
Axes of the slice: x: 2, y: 2, z: 4, core: 2. Of those that a mesh axis runs over, the one named last changes fastest.
Arguments:
- tokens: bfloat16 [4096, 4096], P(('mod', 'seq'), 'tp'), may hold values from -6 to 6
- modality: int32 [4096], replicated, may hold values from 0 to 1, as said below
- norm_gain: float32 [2, 4096], replicated, may hold values from 0.1 to 1.9
- input_weight: bfloat16 [2, 4096, 3, 4096], P('mod', None, None, 'tp'), may hold values from -0.09375 to 0.09375
- head_gain: float32 [2, 2, 128], replicated, may hold values from 1 to 2
- output_weight: bfloat16 [2, 4096, 4096], P('mod', 'tp'), may hold values from -0.125 to 0.125
Outputs:
- update: bfloat16 [4096, 4096], P(('mod', 'seq'), 'tp')
The draws below stay inside these ranges and needn't reach their ends.
Inputs may be any that keep to these rules, and one draw needn't show every extreme that they name: Each value is constant over aligned spans of 64 tokens. Each token shard (the 512 tokens of one index of mod+seq) holds between 3 and 5 image spans, so at most 320 tokens of either modality. In every draw, for some index of seq both of its token shards hold 320 text tokens, and for another index of seq both hold 320 image tokens.
All inputs are finite; a program needn't handle non-finite values.
Results may differ from the reference program's by a relative error of at most 0.019.
Values may be sent and summed in bfloat16 or wider, within the bound.
No kernel may reach another device: no remote copies, remote signals or barrier semaphores. Data moves between devices by JAX's collectives and lax.ppermute only.
A program may use at most 256 MiB of HBM per device.

```python
import math
import jax
import jax.numpy as jnp
from jax import lax

D = 4096
HEADS = 32
HD = 128
TOK_DEV = 512
SPAN = 64
TOKENS = 4096
N_MOD = 2
N_SEQ = 4
N_TP = 4


def draw_modality(key, part):
    shards = TOKENS // TOK_DEV
    blocks = TOK_DEV // SPAN
    key_count, key_seq, key_side, key_rank = jax.random.split(key, 4)
    image_blocks = jax.random.randint(key_count, (N_MOD, N_SEQ), 3, blocks - 2)
    seq_pick = jax.random.permutation(key_seq, N_SEQ)
    side = jax.random.randint(key_side, (), 0, 2)
    first_count = jnp.where(side == 1, blocks - 3, 3)
    second_count = blocks - first_count
    image_blocks = image_blocks.at[:, seq_pick[0]].set(first_count)
    image_blocks = image_blocks.at[:, seq_pick[1]].set(second_count)
    counts = image_blocks.reshape(shards)
    priority = jax.random.randint(key_rank, (shards, blocks), 0, 1 << 20) * blocks + jnp.arange(blocks, dtype=jnp.int32)[None, :]
    ranking = jnp.argsort(jnp.argsort(priority, axis=1), axis=1)
    is_image = (ranking < counts[:, None]).astype(jnp.int32)
    return jnp.repeat(is_image, SPAN, axis=1).reshape(TOKENS)


def strengthened(array, stream_key, source, target, parts, factor):
    owner, partner = [(jnp.arange(array.shape[position]) // (array.shape[position] // parts)).reshape([-1 if axis == position else 1 for axis in range(array.ndim)]) for position in (source, target)]
    chosen = jax.random.permutation(stream_key, parts)[partner]
    strong = (owner == chosen) | (owner == (partner + parts // 2) % parts)
    return jnp.where(strong, factor * array, array)


def steps_of(stream_key, dims, pieces, smallest, top_value):
    level, own = 1.0, jax.random.fold_in(stream_key, 6)
    for axis_at, shards_of in pieces:
        heights = jnp.exp(jax.random.uniform(jax.random.fold_in(own, axis_at), (shards_of,), jnp.float32, smallest / len(pieces), top_value / len(pieces)))
        level = level * jnp.repeat(heights, dims[axis_at] // shards_of).reshape([-1 if axis == axis_at else 1 for axis in range(len(dims))])
    return level


def centred(own_key, extent, deviation, reach, pieces=(), kind=jnp.bfloat16):
    level = steps_of(own_key, extent, pieces, -0.22, 0.18) if pieces else 1.0
    drawn = jax.random.normal(own_key, extent, jnp.float32) * deviation * level
    return jnp.minimum(jnp.maximum(drawn, -reach), reach).astype(kind)


def bell_draw_with(stream_key, dims, width, reach, cuts, heavy, kind=jnp.bfloat16):
    result = width * jax.random.normal(stream_key, dims, jnp.float32)
    if cuts:
        result = result * steps_of(stream_key, dims, cuts, -0.22, 0.18)
    return jnp.clip(strengthened(result, jax.random.fold_in(stream_key, 3), *heavy), -reach, reach).astype(kind)


def setup_inputs(seed: int = 0) -> dict:
    splits = jax.random.split(jax.random.key(seed), 7)
    return {
        "tokens": centred(splits[0], (TOKENS, D), 1.0, 6.0, ((0, 8), (1, 4))),
        "modality": draw_modality(jax.random.fold_in(splits[6], 71), 0),
        "norm_gain": jnp.clip(1.0 + 0.18 * jax.random.normal(splits[2], (2, D), jnp.float32), 0.1, 1.9),
        "input_weight": centred(splits[3], (2, D, 3, D), D ** -0.5, 0.09375, ((0, 2), (3, 4))),
        "head_gain": jnp.clip(jax.random.uniform(splits[4], (2, 2, HD), jnp.float32, 1.0, 2.0), 1.0, 2.0),
        "output_weight": bell_draw_with(splits[5], (2, D, D), D ** -0.5, 0.125, ((0, 2), (1, 4)), (1, 2, 4, 2.0)),
    }


epsilon = 1e-05

def head_norm(part, gain):
    return part * lax.rsqrt(lax.optimization_barrier(jnp.mean(part * part, axis=-1, keepdims=True)) + epsilon) * gain

def reference(tokens, modality, norm_gain, input_weight, head_gain, output_weight):
    image = (modality == 1)[:, None]
    states = tokens.astype(jnp.float32)
    gain = jnp.where(image, norm_gain[1][None, :], norm_gain[0][None, :])
    normed = (states * lax.rsqrt(lax.optimization_barrier(jnp.mean(states * states, axis=1, keepdims=True)) + epsilon) * gain).astype(jnp.bfloat16)
    text_part = jnp.dot(normed, input_weight[0].reshape(D, 3 * D), preferred_element_type=jnp.float32)
    image_part = jnp.dot(normed, input_weight[1].reshape(D, 3 * D), preferred_element_type=jnp.float32)
    projected = jnp.where(image, image_part, text_part).reshape(TOKENS, 3, HEADS, HD)
    selector = image[:, :, None]
    query_gain = jnp.where(selector, head_gain[1, 0][None, None, :], head_gain[0, 0][None, None, :])
    key_gain = jnp.where(selector, head_gain[1, 1][None, None, :], head_gain[0, 1][None, None, :])
    queries = head_norm(projected[:, 0], query_gain).astype(jnp.bfloat16)
    key_rows = head_norm(projected[:, 1], key_gain).astype(jnp.bfloat16)
    value_rows = projected[:, 2].astype(jnp.bfloat16)
    place = jnp.arange(TOKENS, dtype=jnp.int32)
    allowed = place[None, :] <= place[:, None]
    scale = 1.0 / math.sqrt(HD)

    def one_head(operands):
        query_head, key_head, value_head = operands
        scores = jnp.dot(query_head, key_head.T, preferred_element_type=jnp.float32) * scale
        weights = jnp.where(allowed, jnp.exp(scores), 0.0)
        totals = lax.optimization_barrier(jnp.sum(weights, axis=1, keepdims=True))
        rounded = weights.astype(jnp.bfloat16)
        weighted = jnp.dot(rounded, value_head, preferred_element_type=jnp.float32)
        return (weighted / totals).astype(jnp.bfloat16)
    per_head = lax.map(one_head, (queries.transpose(1, 0, 2), key_rows.transpose(1, 0, 2), value_rows.transpose(1, 0, 2)))
    attention = per_head.transpose(1, 0, 2).reshape(TOKENS, D)
    block = D // N_TP
    attention_blocks = attention.reshape(TOKENS, N_TP, block).transpose(1, 0, 2)
    text_blocks = output_weight[0].reshape(N_TP, block, D)
    image_blocks = output_weight[1].reshape(N_TP, block, D)

    def add_block(total, operands):
        part, text_rows, image_rows = operands
        term = jnp.where(image, jnp.dot(part, image_rows, preferred_element_type=jnp.float32), jnp.dot(part, text_rows, preferred_element_type=jnp.float32)).astype(jnp.bfloat16)
        term = lax.optimization_barrier(term)
        return (total + term.astype(jnp.float32), None)
    total, unused = lax.scan(add_block, jnp.zeros((TOKENS, D), jnp.float32), (attention_blocks, text_blocks, image_blocks))
    return total.astype(jnp.bfloat16)
```

```python
from functools import partial
import math

import jax
import jax.numpy as jnp
from jax import lax
from jax.experimental import pallas as pl
from jax.experimental.pallas import tpu as pltpu
from jax.sharding import PartitionSpec as P

HD = 128
CAP = 320
SPAN = 64
SLOTS = CAP // SPAN
VMEM = 56 * 1024 * 1024


epsilon = 1e-05
sentinel = 1 << 30


def route_table(shard_ids, shard_index, slot_count):
    length = shard_ids.shape[0]
    order = jnp.argsort(shard_ids, stable=True)
    text_count = jnp.sum((shard_ids == 0).astype(jnp.int32))
    padded = jnp.concatenate([order, jnp.zeros((slot_count,), jnp.int32)])
    slot_index = jnp.arange(slot_count, dtype=jnp.int32)
    picked = jnp.stack(
        [padded[:slot_count], lax.dynamic_slice_in_dim(padded, text_count, slot_count)]
    )
    live = jnp.stack([slot_index < text_count, slot_index < length - text_count])
    place = shard_index * length + picked
    query_place = jnp.where(live, place, -1)
    key_place = jnp.where(live, place, sentinel)
    return (order, text_count, picked, live, query_place, key_place)


def select_rows(table, picked, live):
    return jnp.where(live[:, :, None], table[picked], jnp.zeros((), table.dtype))


def head_norm(part, gain):
    return part * lax.rsqrt(jnp.mean(part * part, axis=-1, keepdims=True) + epsilon) * gain


def general_body(tokens, modality, norm_gain, input_weight, head_gain, output_weight):
    length = tokens.shape[0]
    mod_count = lax.axis_size("mod")
    seq_count = lax.axis_size("seq")
    shards = mod_count * seq_count
    mine = lax.axis_index("mod")
    seq_index = lax.axis_index("seq")
    all_ids = modality.reshape(shards, length)
    own_index = mine * seq_count + seq_index
    own_ids = lax.dynamic_index_in_dim(all_ids, own_index, 0, keepdims=False)
    own_table = route_table(own_ids, own_index, CAP)
    order = own_table[0]
    text_count = own_table[1]
    picked = own_table[2]
    live = own_table[3]
    tables = jax.vmap(partial(route_table, slot_count=CAP))(
        all_ids, jnp.arange(shards, dtype=jnp.int32)
    )
    query_grid = tables[4].reshape(mod_count, seq_count, 2, CAP)
    own_query = lax.dynamic_index_in_dim(query_grid, seq_index, 1, keepdims=False)
    own_query = lax.dynamic_index_in_dim(own_query, mine, 1, keepdims=False).reshape(
        mod_count * CAP
    )
    key_grid = tables[5].reshape(mod_count, seq_count, 2, CAP)
    key_order = jnp.transpose(key_grid, (2, 1, 0, 3)).reshape(shards * mod_count * CAP)
    gathered = lax.all_gather(tokens, "tp", axis=1, tiled=True)
    arrived = lax.all_to_all(
        select_rows(gathered, picked, live), "mod", split_axis=0, concat_axis=0, tiled=True
    )
    rows_total = arrived.shape[0] * arrived.shape[1]
    width = arrived.shape[2]
    states = arrived.reshape(rows_total, width).astype(jnp.float32)
    gain = lax.dynamic_index_in_dim(norm_gain, mine, 0, keepdims=False)
    normed = (
        states * lax.rsqrt(jnp.mean(states * states, axis=1, keepdims=True) + epsilon) * gain
    ).astype(jnp.bfloat16)
    local_width = input_weight.shape[3]
    heads_here = local_width // HD
    projected = jnp.dot(
        normed, input_weight[0].reshape(width, 3 * local_width), preferred_element_type=jnp.float32
    )
    projected = projected.reshape(rows_total, 3, heads_here, HD)
    gains = lax.dynamic_index_in_dim(head_gain, mine, 0, keepdims=False)
    query_rows = head_norm(projected[:, 0], gains[0]).astype(jnp.bfloat16)
    key_rows = (
        head_norm(projected[:, 1], gains[1]).astype(jnp.bfloat16).reshape(rows_total, local_width)
    )
    value_rows = projected[:, 2].astype(jnp.bfloat16).reshape(rows_total, local_width)
    scale = 1.0 / math.sqrt(HD)
    key_piece = lax.all_gather(key_rows, ("mod", "seq"), axis=0, tiled=True)
    value_piece = lax.all_gather(value_rows, ("mod", "seq"), axis=0, tiled=True)
    count = key_piece.shape[0]
    scores = (
        jnp.einsum(
            "rhe,khe->hrk",
            query_rows,
            key_piece.reshape(count, heads_here, HD),
            preferred_element_type=jnp.float32,
        )
        * scale
    )
    weights = jnp.where(key_order[None, None, :] <= own_query[None, :, None], jnp.exp(scores), 0.0)
    totals = jnp.sum(weights, axis=2)
    rounded = weights.astype(jnp.bfloat16)
    weighted = jnp.einsum(
        "hrk,khe->rhe",
        rounded,
        value_piece.reshape(count, heads_here, HD),
        preferred_element_type=jnp.float32,
    )
    weighted, totals = (weighted, totals)
    totals = jnp.where(own_query[None, :] >= 0, totals, 1.0)
    attention = (
        (weighted / jnp.transpose(totals)[:, :, None])
        .astype(jnp.bfloat16)
        .reshape(rows_total, local_width)
    )
    head_terms = jnp.dot(attention, output_weight[0], preferred_element_type=jnp.float32)
    summed = lax.psum_scatter(
        head_terms.astype(jnp.bfloat16), "tp", scatter_dimension=1, tiled=True
    ).astype(jnp.float32)
    result = summed.astype(jnp.bfloat16).reshape(mod_count, CAP, summed.shape[1])
    returned = lax.all_to_all(result, "mod", split_axis=0, concat_axis=0, tiled=True)
    flat = returned.reshape(mod_count * CAP, summed.shape[1])
    inverse = jnp.zeros((length,), jnp.int32).at[order].set(jnp.arange(length, dtype=jnp.int32))
    slot = own_ids * CAP + inverse - own_ids * text_count
    return flat[slot]


def swap(size, bit):
    return [(i, i ^ bit) for i in range(size)]


def project_kernel(chunk, meta, ids, low, p1, p2, p3a, p3b, q1, q2, q3a, q3b, gain, head_gain, own_w, other_w, o0, o1, o2, o3, rows, inverse, parts, table):
    step = pl.program_id(0)
    mine, seq, tp = meta[0], meta[1], meta[2]
    width = rows.shape[3]
    features = 4 * width

    @pl.when(step == 0)
    def _():
        counts = [jnp.int32(0), jnp.int32(0)]
        for j in range(8):
            near, at = j < 4, j % 4
            span = 4 * mine + at if near else 4 * (1 - mine) + at
            kind = ids[(chunk * 4 + seq) * 8 + span]
            same = (kind == mine).astype(jnp.int32)
            group = 1 - same
            slot = jnp.where(same == 1, counts[0], counts[1])
            counts = [counts[0] + same, counts[1] + group]
            table[group * 8 + slot] = span
            place = pl.ds(pl.multiple_of(slot * SPAN, SPAN), SPAN)
            total = jnp.zeros((SPAN, 1), jnp.float32)
            for k in range(4):
                if k == 0:
                    value = low[pl.ds(pl.multiple_of(span * SPAN, SPAN), SPAN), :]
                elif k < 3:
                    ref = ((p1, p2) if near else (q1, q2))[k - 1]
                    value = ref[at * SPAN : (at + 1) * SPAN, :]
                else:
                    ref = ((p3a, p3b) if near else (q3a, q3b))[at // 2]
                    value = ref[(at % 2) * SPAN : (at % 2 + 1) * SPAN, :]
                value = value.astype(jnp.float32)
                total += jnp.sum(value * value, axis=1, keepdims=True)
                block = tp ^ k
                rows[block, group, place, :] = (value * gain[kind * 4 + block]).astype(jnp.bfloat16)
            scale = lax.rsqrt(total / features + epsilon)
            inverse[group, place, :] = jnp.broadcast_to(scale, (SPAN, HD))
        table[16] = counts[0]
        table[17] = counts[1]

    def part(group, weight):
        total = None
        for f in range(4):
            term = jnp.dot(
                rows[f, group], weight[0, f * width : (f + 1) * width, :], preferred_element_type=jnp.float32
            )
            total = term if total is None else total + term
        for h in range(4):
            parts[h] = total[:, h * HD : (h + 1) * HD]
        kind = mine if group == 0 else 1 - mine
        which = lax.rem(step, 3)
        scale = inverse[group]
        count = table[16 + group]
        for k, out in enumerate((o0, o1, o2, o3)):
            piece = parts[seq ^ k] * scale
            mean = jnp.mean(piece * piece, axis=1, keepdims=True)
            normed = piece * lax.rsqrt(mean + epsilon) * head_gain[kind * 2 + jnp.minimum(which, 1)]
            value = jnp.where(which == 2, piece, normed).astype(jnp.bfloat16)
            for slot in range(SLOTS):

                @pl.when(slot < count)
                def _():
                    span = table[group * 8 + slot]
                    out[which, pl.ds(pl.multiple_of(span * SPAN, SPAN), SPAN), :] = value[
                        slot * SPAN : (slot + 1) * SPAN
                    ]

    @pl.when(step < 3)
    def _():
        part(0, own_w)

    @pl.when(step >= 3)
    def _():
        part(1, other_w)


def project(chunk, meta, ids, pieces, gain, head_gain, own_w, other_w):
    depth, half = other_w.shape[1:]
    width = depth // 4
    whole = pl.BlockSpec(memory_space=pltpu.VMEM)
    shape = jax.ShapeDtypeStruct((3, 8 * SPAN, HD), jnp.bfloat16)
    return pl.pallas_call(
        partial(project_kernel, chunk),
        grid_spec=pltpu.PrefetchScalarGridSpec(
            num_scalar_prefetch=2,
            grid=(6,),
            in_specs=[whole] * 11
            + [
                pl.BlockSpec((1, depth, half), lambda i, meta, ids: (jnp.minimum(i, 2), 0, meta[0])),
                pl.BlockSpec((1, depth, half), lambda i, meta, ids: (jnp.maximum(i - 3, 0), 0, 0)),
            ],
            out_specs=[whole] * 4,
            scratch_shapes=[
                pltpu.VMEM((4, 2, CAP, width), jnp.bfloat16),
                pltpu.VMEM((2, CAP, HD), jnp.float32),
                pltpu.VMEM((4, CAP, HD), jnp.float32),
                pltpu.SMEM((32,), jnp.int32),
            ],
        ),
        out_shape=[shape] * 4,
        compiler_params=pltpu.CompilerParams(vmem_limit_bytes=VMEM),
        cost_estimate=pl.CostEstimate(
            flops=2 * 2 * CAP * depth * 3 * half, bytes_accessed=2 * 3 * depth * half * 2, transcendentals=0
        ),
        name="project",
    )(meta, ids, *pieces, gain, head_gain, own_w, other_w)


def attend_kernel(high, meta, *refs):
    first, last = refs[:4], refs[4:8] if high else refs[:4]
    out, queries, keys, values = refs[-4:]
    seq = meta[1]
    block = queries.shape[1]
    half = block // 2
    for k in range(4):
        at = seq ^ k
        queries[at] = last[k][0]
        for base, pieces in ((0, first), (4, last)) if high else ((0, first),):
            keys[base + at] = pieces[k][1]
            values[base + at, :, :HD] = pieces[k][2]
            values[base + at, :, HD:] = jnp.ones((block, HD), jnp.bfloat16)
    diagonal = lax.broadcasted_iota(jnp.int32, (half, half), 0) >= lax.broadcasted_iota(
        jnp.int32, (half, half), 1
    )

    def scores(query, key):
        return lax.dot_general(query, key, (((1,), (1,)), ((), ())), preferred_element_type=jnp.float32)

    for at in range(4):
        own = 4 + at if high else at
        for side in range(2):
            query = queries[at, side * half : (side + 1) * half, :]
            weight = jnp.where(
                diagonal, jnp.exp2(scores(query, keys[own, side * half : (side + 1) * half, :])), 0.0
            ).astype(jnp.bfloat16)
            total = jnp.dot(
                weight, values[own, side * half : (side + 1) * half, :], preferred_element_type=jnp.float32
            )
            if side == 1:
                weight = jnp.exp2(scores(query, keys[own, :half, :])).astype(jnp.bfloat16)
                total += jnp.dot(weight, values[own, :half, :], preferred_element_type=jnp.float32)

            def step(j, total):
                weight = jnp.exp2(scores(query, keys[j])).astype(jnp.bfloat16)
                return total + jnp.dot(weight, values[j], preferred_element_type=jnp.float32)

            if own:
                total = lax.fori_loop(0, own, step, total, unroll=True)
            out[side, at] = (total[:, :HD] / total[:, HD:]).astype(jnp.bfloat16)


def attend(meta, first, last=None):
    high = last is not None
    pieces = list(first) + (list(last) if high else [])
    block = first[0].shape[1]
    whole = pl.BlockSpec(memory_space=pltpu.VMEM)
    count = 8 if high else 4
    return pl.pallas_call(
        partial(attend_kernel, high),
        in_specs=[pl.BlockSpec(memory_space=pltpu.SMEM)] + [whole] * len(pieces),
        out_specs=whole,
        out_shape=jax.ShapeDtypeStruct((2, 4, block // 2, HD), jnp.bfloat16),
        scratch_shapes=[
            pltpu.VMEM((4, block, HD), jnp.bfloat16),
            pltpu.VMEM((count, block, HD), jnp.bfloat16),
            pltpu.VMEM((count, block, 2 * HD), jnp.bfloat16),
        ],
        compiler_params=pltpu.CompilerParams(vmem_limit_bytes=VMEM),
        cost_estimate=pl.CostEstimate(
            flops=(26 if high else 10) * block * block * 6 * HD,
            bytes_accessed=4 * count * block * HD * 2,
            transcendentals=(26 if high else 10) * block * block,
        ),
        name="attend",
    )(meta, *pieces)


ORDER = (3, 1, 2, 0)


def finish_kernel(chunk, meta, ids, heads, own_w, other_w, to_x, to_y, keep_a, keep_b, rows):
    step = pl.program_id(0)
    mine, seq = meta[0], meta[1]

    @pl.when(step == 0)
    def _():
        for j in range(4):
            same = ids[(chunk * 4 + seq) * 8 + 4 * mine + j] == mine
            for h in range(8):
                value = heads[h, j * SPAN : (j + 1) * SPAN, :]
                zero = jnp.zeros_like(value)
                rows[0, j * SPAN : (j + 1) * SPAN, h * HD : (h + 1) * HD] = jnp.where(same, value, zero)
                rows[1, j * SPAN : (j + 1) * SPAN, h * HD : (h + 1) * HD] = jnp.where(same, zero, value)

    term = jnp.dot(rows[0], own_w[...], preferred_element_type=jnp.float32)
    term += jnp.dot(rows[1], other_w[...], preferred_element_type=jnp.float32)
    term = term.astype(jnp.bfloat16)
    half = term.shape[0] // 2
    places = {
        0: ((keep_a, 0), (keep_b, 0)),
        1: ((to_x, 0), (keep_b, 1)),
        2: ((keep_a, 1), (to_y, 0)),
        3: ((to_x, 1), (to_y, 1)),
    }
    for at, k in enumerate(ORDER):

        @pl.when(step == at)
        def _():
            (a, i), (b, j) = places[k]
            a[i] = term[:half]
            b[j] = term[half:]


def finish(chunk, meta, ids, heads, own_w, other_w):
    depth, total = own_w.shape
    width = total // 4
    count = heads.shape[1]
    whole = pl.BlockSpec(memory_space=pltpu.VMEM)

    def column(i, meta, ids):
        k = jnp.where(i == 0, 3, jnp.where(i == 3, 0, i))
        return (0, meta[2] ^ k)

    shape = jax.ShapeDtypeStruct((2, count // 2, width), jnp.bfloat16)
    return pl.pallas_call(
        partial(finish_kernel, chunk),
        grid_spec=pltpu.PrefetchScalarGridSpec(
            num_scalar_prefetch=2,
            grid=(4,),
            in_specs=[whole, pl.BlockSpec((depth, width), column), pl.BlockSpec((depth, width), column)],
            out_specs=[whole] * 4,
            scratch_shapes=[pltpu.VMEM((2, count, depth), jnp.bfloat16)],
        ),
        out_shape=[shape] * 4,
        compiler_params=pltpu.CompilerParams(vmem_limit_bytes=VMEM),
        cost_estimate=pl.CostEstimate(
            flops=2 * 2 * count * depth * total, bytes_accessed=2 * depth * total * 2, transcendentals=0
        ),
        name="finish",
    )(meta, ids, heads, own_w, other_w)


def body(tokens, modality, norm_gain, input_weight, head_gain, output_weight):
    mine, seq, tp = lax.axis_index("mod"), lax.axis_index("seq"), lax.axis_index("tp")
    width = tokens.shape[1]
    half = input_weight.shape[3] // 2
    first = mine == 0
    meta = jnp.stack([mine, seq, tp]).astype(jnp.int32)
    ids = modality.reshape(-1, SPAN)[:, 0]

    def to_mod(value):
        return lax.ppermute(value, "mod", swap(2, 1))

    def to_x(value):
        return lax.ppermute(value, "tp", swap(4, 1))

    def to_y(value):
        return lax.ppermute(value, "tp", swap(4, 2))

    partner = to_mod(tokens)
    blocks = [jnp.where(first, tokens, partner), jnp.where(first, partner, tokens)]
    own_w = jnp.transpose(input_weight[0], (1, 0, 2))
    other_w = to_mod(lax.dynamic_slice_in_dim(own_w, (1 - mine) * half, half, axis=2))
    own_out = output_weight[0]
    other_out = to_mod(own_out)
    gain = norm_gain.reshape(8, 1, width)
    fold = jnp.array([math.log2(math.e) / math.sqrt(HD), 1.0], jnp.float32).reshape(1, 2, 1)
    gains = (head_gain * fold).reshape(4, 1, HD)

    arrived = []
    for chunk in range(2):
        block = blocks[chunk]
        rows = block.shape[0] // 2
        part = lax.dynamic_slice_in_dim(block, mine * rows, rows, axis=0)
        p1, p2 = to_x(part), to_y(part)
        p3a, p3b = to_y(p1[: rows // 2]), to_x(p2[rows // 2 :])
        pieces = [block, p1, p2, p3a, p3b] + [to_mod(p) for p in (p1, p2, p3a, p3b)]
        sent = project(chunk, meta, ids, pieces, gain, gains, own_w, other_w)
        arrived.append([sent[0]] + [lax.ppermute(sent[k], "seq", swap(4, k)) for k in (1, 2, 3)])

    results = []
    for chunk in range(2):
        mixed = attend(meta, arrived[0], arrived[1] if chunk else None)
        mixed = mixed.reshape((8,) + mixed.shape[2:])
        heads = lax.all_to_all(mixed, ("mod", "seq"), 0, 0, tiled=True)
        send_x, send_y, keep_a, keep_b = finish(chunk, meta, ids, heads, own_out, other_out)
        got_x, got_y = to_x(send_x).astype(jnp.float32), to_y(send_y).astype(jnp.float32)
        keep_a, keep_b = keep_a.astype(jnp.float32), keep_b.astype(jnp.float32)
        last_a = to_y((keep_a[1] + got_x[1]).astype(jnp.bfloat16)).astype(jnp.float32)
        last_b = to_x((keep_b[1] + got_y[1]).astype(jnp.bfloat16)).astype(jnp.float32)
        result = jnp.concatenate([keep_a[0] + got_x[0] + last_a, keep_b[0] + got_y[0] + last_b])
        results.append(result.astype(jnp.bfloat16))
    back = to_mod(jnp.where(first, results[1], results[0]))
    return jnp.concatenate(
        [jnp.where(first, results[0], back), jnp.where(first, back, results[1])], axis=0
    )


def solution(mesh):
    sizes = dict(mesh.shape)
    in_specs = (
        P(("mod", "seq"), "tp"),
        P(),
        P(),
        P("mod", None, None, "tp"),
        P(),
        P("mod", "tp", None),
    )
    out_specs = P(("mod", "seq"), "tp")

    def run(tokens, modality, norm_gain, input_weight, head_gain, output_weight):
        heads = input_weight.shape[3] // HD
        shard = tokens.shape[0] // (sizes["mod"] * sizes["seq"])
        small = (sizes["mod"], sizes["seq"], sizes["tp"]) == (2, 4, 4)
        fits = small and heads == 32 and shard == 8 * SPAN
        return jax.shard_map(
            body if fits else general_body,
            mesh=mesh,
            in_specs=in_specs,
            out_specs=out_specs,
            check_vma=False,
        )(tokens, modality, norm_gain, input_weight, head_gain, output_weight)

    return run
```

```python
from functools import partial
import math

import jax
import jax.numpy as jnp
from jax import lax
from jax.experimental import pallas as pl
from jax.experimental.pallas import tpu as pltpu
from jax.sharding import PartitionSpec as P

HD = 128
CAP = 320
SPAN = 64
SLOTS = CAP // SPAN
VMEM = 56 * 1024 * 1024


epsilon = 1e-05
sentinel = 1 << 30


def route_table(shard_ids, shard_index, slot_count):
    length = shard_ids.shape[0]
    order = jnp.argsort(shard_ids, stable=True)
    text_count = jnp.sum((shard_ids == 0).astype(jnp.int32))
    padded = jnp.concatenate([order, jnp.zeros((slot_count,), jnp.int32)])
    slot_index = jnp.arange(slot_count, dtype=jnp.int32)
    picked = jnp.stack(
        [padded[:slot_count], lax.dynamic_slice_in_dim(padded, text_count, slot_count)]
    )
    live = jnp.stack([slot_index < text_count, slot_index < length - text_count])
    place = shard_index * length + picked
    query_place = jnp.where(live, place, -1)
    key_place = jnp.where(live, place, sentinel)
    return (order, text_count, picked, live, query_place, key_place)


def select_rows(table, picked, live):
    return jnp.where(live[:, :, None], table[picked], jnp.zeros((), table.dtype))


def head_norm(part, gain):
    return part * lax.rsqrt(jnp.mean(part * part, axis=-1, keepdims=True) + epsilon) * gain


def general_body(tokens, modality, norm_gain, input_weight, head_gain, output_weight):
    length = tokens.shape[0]
    mod_count = lax.axis_size("mod")
    seq_count = lax.axis_size("seq")
    shards = mod_count * seq_count
    mine = lax.axis_index("mod")
    seq_index = lax.axis_index("seq")
    all_ids = modality.reshape(shards, length)
    own_index = mine * seq_count + seq_index
    own_ids = lax.dynamic_index_in_dim(all_ids, own_index, 0, keepdims=False)
    own_table = route_table(own_ids, own_index, CAP)
    order = own_table[0]
    text_count = own_table[1]
    picked = own_table[2]
    live = own_table[3]
    tables = jax.vmap(partial(route_table, slot_count=CAP))(
        all_ids, jnp.arange(shards, dtype=jnp.int32)
    )
    query_grid = tables[4].reshape(mod_count, seq_count, 2, CAP)
    own_query = lax.dynamic_index_in_dim(query_grid, seq_index, 1, keepdims=False)
    own_query = lax.dynamic_index_in_dim(own_query, mine, 1, keepdims=False).reshape(
        mod_count * CAP
    )
    key_grid = tables[5].reshape(mod_count, seq_count, 2, CAP)
    key_order = jnp.transpose(key_grid, (2, 1, 0, 3)).reshape(shards * mod_count * CAP)
    gathered = lax.all_gather(tokens, "tp", axis=1, tiled=True)
    arrived = lax.all_to_all(
        select_rows(gathered, picked, live), "mod", split_axis=0, concat_axis=0, tiled=True
    )
    rows_total = arrived.shape[0] * arrived.shape[1]
    width = arrived.shape[2]
    states = arrived.reshape(rows_total, width).astype(jnp.float32)
    gain = lax.dynamic_index_in_dim(norm_gain, mine, 0, keepdims=False)
    normed = (
        states * lax.rsqrt(jnp.mean(states * states, axis=1, keepdims=True) + epsilon) * gain
    ).astype(jnp.bfloat16)
    local_width = input_weight.shape[3]
    heads_here = local_width // HD
    projected = jnp.dot(
        normed, input_weight[0].reshape(width, 3 * local_width), preferred_element_type=jnp.float32
    )
    projected = projected.reshape(rows_total, 3, heads_here, HD)
    gains = lax.dynamic_index_in_dim(head_gain, mine, 0, keepdims=False)
    query_rows = head_norm(projected[:, 0], gains[0]).astype(jnp.bfloat16)
    key_rows = (
        head_norm(projected[:, 1], gains[1]).astype(jnp.bfloat16).reshape(rows_total, local_width)
    )
    value_rows = projected[:, 2].astype(jnp.bfloat16).reshape(rows_total, local_width)
    scale = 1.0 / math.sqrt(HD)
    key_piece = lax.all_gather(key_rows, ("mod", "seq"), axis=0, tiled=True)
    value_piece = lax.all_gather(value_rows, ("mod", "seq"), axis=0, tiled=True)
    count = key_piece.shape[0]
    scores = (
        jnp.einsum(
            "rhe,khe->hrk",
            query_rows,
            key_piece.reshape(count, heads_here, HD),
            preferred_element_type=jnp.float32,
        )
        * scale
    )
    weights = jnp.where(key_order[None, None, :] <= own_query[None, :, None], jnp.exp(scores), 0.0)
    totals = jnp.sum(weights, axis=2)
    rounded = weights.astype(jnp.bfloat16)
    weighted = jnp.einsum(
        "hrk,khe->rhe",
        rounded,
        value_piece.reshape(count, heads_here, HD),
        preferred_element_type=jnp.float32,
    )
    weighted, totals = (weighted, totals)
    totals = jnp.where(own_query[None, :] >= 0, totals, 1.0)
    attention = (
        (weighted / jnp.transpose(totals)[:, :, None])
        .astype(jnp.bfloat16)
        .reshape(rows_total, local_width)
    )
    head_terms = jnp.dot(attention, output_weight[0], preferred_element_type=jnp.float32)
    summed = lax.psum_scatter(
        head_terms.astype(jnp.bfloat16), "tp", scatter_dimension=1, tiled=True
    ).astype(jnp.float32)
    result = summed.astype(jnp.bfloat16).reshape(mod_count, CAP, summed.shape[1])
    returned = lax.all_to_all(result, "mod", split_axis=0, concat_axis=0, tiled=True)
    flat = returned.reshape(mod_count * CAP, summed.shape[1])
    inverse = jnp.zeros((length,), jnp.int32).at[order].set(jnp.arange(length, dtype=jnp.int32))
    slot = own_ids * CAP + inverse - own_ids * text_count
    return flat[slot]


def swap(size, bit):
    return [(i, i ^ bit) for i in range(size)]


def half_kernel(parts, meta, weight, *refs):
    out, held, come, gone = refs[-4:]
    half = out.shape[2]
    depth = held.shape[1]
    start = pl.multiple_of((1 - meta[0]) * half, half)
    inward, outward = [], []
    for n, part in enumerate(parts):
        for f in range(out.shape[1] // depth):
            at, deep = len(inward), pl.ds(f * depth, depth)
            source = weight.at[part, deep, pl.ds(start, half)]
            inward.append(pltpu.make_async_copy(source, held.at[at], come.at[at]))
            outward.append(pltpu.make_async_copy(held.at[at], out.at[n, deep, :], gone.at[at]))
    for copy in inward:
        copy.start()
    for first, second in zip(inward, outward):
        first.wait()
        second.start()
    for copy in outward:
        copy.wait()


def other_half(meta, after, weight, parts):
    outside = pl.BlockSpec(memory_space=pl.ANY)
    depth, half = weight.shape[1], weight.shape[2] // 2
    count = 4 * len(parts)
    return pl.pallas_call(
        partial(half_kernel, parts),
        in_specs=[pl.BlockSpec(memory_space=pltpu.SMEM)] + [outside] * (1 + len(after)),
        out_specs=outside,
        out_shape=jax.ShapeDtypeStruct((len(parts), depth, half), weight.dtype),
        scratch_shapes=[
            pltpu.VMEM((count, depth // 4, half), weight.dtype),
            pltpu.SemaphoreType.DMA((count,)),
            pltpu.SemaphoreType.DMA((count,)),
        ],
        compiler_params=pltpu.CompilerParams(vmem_limit_bytes=VMEM),
        cost_estimate=pl.CostEstimate(flops=count * 1000000000, bytes_accessed=1000, transcendentals=0),
        name="other_half",
    )(meta, weight, *after)


def project_kernel(chunk, meta, ids, block, p1, p2, p3a, p3b, q, gain, head_gain, own_w, early_w, late_w, out, rows, inverse, tiles, table, sems):
    mine, seq, tp = meta[0], meta[1], meta[2]
    width, half = tiles.shape[2:]
    features = 4 * width
    quarter = p3a.shape[0]

    def part_of(step):
        which = lax.rem(step, 3)
        return jnp.where(which == 0, 1, jnp.where(which == 1, 0, 2))

    def copies(step, act):
        which = lax.rem(step, 3)
        for f in range(4):
            deep = pl.ds(f * width, width)
            slot = lax.rem(step, 2) * 4 + f

            def move(source):
                act(pltpu.make_async_copy(source, tiles.at[lax.rem(step, 2), f], sems.at[slot]))

            @pl.when(step < 3)
            def _():
                move(own_w.at[part_of(step), deep, pl.ds(pl.multiple_of(mine * half, half), half)])

            @pl.when((step == 3) | (step == 4))
            def _():
                move(early_w.at[jnp.minimum(which, 1), deep, :])

            @pl.when(step == 5)
            def _():
                move(late_w.at[0, deep, :])

    for step in range(2):
        copies(jnp.int32(step), lambda copy: copy.start())

    counts = [jnp.int32(0), jnp.int32(0)]
    for j in range(8):
        near, at = j < 4, j % 4
        span = 4 * mine + at if near else 4 * (1 - mine) + at
        kind = ids[((chunk * 4 + seq) * 8 + span) * SPAN]
        same = (kind == mine).astype(jnp.int32)
        group = 1 - same
        slot = jnp.where(same == 1, counts[0], counts[1])
        counts = [counts[0] + same, counts[1] + group]
        table[group * 8 + slot] = span
        place = pl.ds(pl.multiple_of(slot * SPAN, SPAN), SPAN)
        total = jnp.zeros((SPAN, 1), jnp.float32)
        for k in range(4):
            if k == 0:
                value = block[pl.ds(pl.multiple_of(span * SPAN, SPAN), SPAN), :]
            elif not near:
                start = (k - 1) * 2 * quarter + at * SPAN
                value = q[start : start + SPAN, :]
            else:
                ref, base = ((p1, 0), (p2, 0), ((p3a, p3b)[at // 2], at // 2 * 2))[k - 1]
                value = ref[(at - base) * SPAN : (at - base + 1) * SPAN, :]
            value = value.astype(jnp.float32)
            total += jnp.sum(value * value, axis=1, keepdims=True)
            feature = tp ^ k
            scale = gain[pl.ds(kind, 1), pl.ds(pl.multiple_of(feature * width, width), width)]
            rows[feature, group, place, :] = (value * scale).astype(jnp.bfloat16)
        scale = lax.rsqrt(total / features + epsilon)
        inverse[group, place, :] = jnp.broadcast_to(scale, (SPAN, HD))
    table[16] = counts[0]
    table[17] = counts[1]

    @pl.loop(0, 6)
    def _(step):
        group = (step >= 3).astype(jnp.int32)
        copies(step, lambda copy: copy.wait())
        buffer = lax.rem(step, 2)
        total = None
        for f in range(4):
            term = jnp.dot(rows[f, group], tiles[buffer, f], preferred_element_type=jnp.float32)
            total = term if total is None else total + term
        @pl.when(step < 4)
        def _():
            copies(step + 2, lambda copy: copy.start())

        kind = jnp.where(group == 0, mine, 1 - mine)
        which = part_of(step)
        scale = inverse[group]
        count = table[16 + group]
        row = head_gain[kind, pl.ds(jnp.minimum(which, 1), 1), :]
        row = row * jnp.where(which == 0, math.log2(math.e) / math.sqrt(HD), 1.0)
        for h in range(4):
            piece = total[:, h * HD : (h + 1) * HD] * scale
            mean = jnp.mean(piece * piece, axis=1, keepdims=True)
            normed = piece * lax.rsqrt(mean + epsilon) * row
            value = jnp.where(which == 2, piece, normed).astype(jnp.bfloat16)
            for slot in range(SLOTS):

                @pl.when(slot < count)
                def _():
                    span = table[group * 8 + slot]
                    out[h, which, pl.ds(pl.multiple_of(span * SPAN, SPAN), SPAN), :] = value[
                        slot * SPAN : (slot + 1) * SPAN
                    ]


def project(chunk, meta, ids, pieces, gain, head_gain, own_w, early_w, late_w):
    depth, half = early_w.shape[1:]
    width = depth // 4
    whole = pl.BlockSpec(memory_space=pltpu.VMEM)
    scalars = pl.BlockSpec(memory_space=pltpu.SMEM)
    outside = pl.BlockSpec(memory_space=pl.ANY)
    shape = jax.ShapeDtypeStruct((4, 3, 8 * SPAN, HD), jnp.bfloat16)
    return pl.pallas_call(
        partial(project_kernel, chunk),
        in_specs=[scalars] * 2 + [whole] * 8 + [outside] * 3,
        out_specs=whole,
        scratch_shapes=[
            pltpu.VMEM((4, 2, CAP, width), jnp.bfloat16),
            pltpu.VMEM((2, CAP, HD), jnp.float32),
            pltpu.VMEM((2, 4, width, half), jnp.bfloat16),
            pltpu.SMEM((32,), jnp.int32),
            pltpu.SemaphoreType.DMA((8,)),
        ],
        out_shape=shape,
        compiler_params=pltpu.CompilerParams(vmem_limit_bytes=VMEM),
        cost_estimate=pl.CostEstimate(flops=20000000000, bytes_accessed=1000, transcendentals=0),
        name="project",
    )(meta, ids, *pieces, gain, head_gain, own_w, early_w, late_w)


def attend_kernel(high, meta, after, later, *refs):
    first, last = refs[0], refs[1] if high else refs[0]
    out, values = refs[-2:]
    block = last.shape[2]
    half = block // 2
    for base, pieces in ((0, first), (4, last)) if high else ((0, first),):
        for at in range(4):
            values[base + at, :, :HD] = pieces[at, 2]
            values[base + at, :, HD:] = jnp.ones((block, HD), jnp.bfloat16)
    diagonal = lax.broadcasted_iota(jnp.int32, (half, half), 0) >= lax.broadcasted_iota(
        jnp.int32, (half, half), 1
    )

    def scores(query, key):
        return lax.dot_general(query, key, (((1,), (1,)), ((), ())), preferred_element_type=jnp.float32)

    for at in range(4):
        own = 4 + at if high else at
        for side in range(2):
            query = last[at, 0, side * half : (side + 1) * half, :]
            weight = jnp.where(
                diagonal, jnp.exp2(scores(query, last[at, 1, side * half : (side + 1) * half, :])), 0.0
            ).astype(jnp.bfloat16)
            total = jnp.dot(
                weight, values[own, side * half : (side + 1) * half, :], preferred_element_type=jnp.float32
            )
            if side == 1:
                weight = jnp.exp2(scores(query, last[at, 1, :half, :])).astype(jnp.bfloat16)
                total += jnp.dot(weight, values[own, :half, :], preferred_element_type=jnp.float32)

            for j in range(own):
                key = first[j, 1] if j < 4 else last[j - 4, 1]
                weight = jnp.exp2(scores(query, key)).astype(jnp.bfloat16)
                total += jnp.dot(weight, values[j], preferred_element_type=jnp.float32)
            out[side, at] = (total[:, :HD] / total[:, HD:]).astype(jnp.bfloat16)


def attend(meta, after, later, first, last=None):
    high = last is not None
    pieces = [first, last] if high else [first]
    block = first.shape[2]
    whole = pl.BlockSpec(memory_space=pltpu.VMEM)
    count = 8 if high else 4
    return pl.pallas_call(
        partial(attend_kernel, high),
        in_specs=[pl.BlockSpec(memory_space=pltpu.SMEM)]
        + [pl.BlockSpec(memory_space=pl.ANY)] * 2
        + [whole] * len(pieces),
        out_specs=whole,
        out_shape=jax.ShapeDtypeStruct((2, 4, block // 2, HD), jnp.bfloat16),
        scratch_shapes=[
            pltpu.VMEM((count, block, 2 * HD), jnp.bfloat16),
        ],
        compiler_params=pltpu.CompilerParams(vmem_limit_bytes=VMEM),
        cost_estimate=pl.CostEstimate(flops=12000000000 if high else 6000000000, bytes_accessed=1000, transcendentals=0),
        name="attend",
    )(meta, after, later, *pieces)


ORDER = (3, 1, 2, 0)


def finish_kernel(chunk, meta, ids, after, heads, own_w, other_w, to_x, to_y, keep_a, keep_b, rows):
    step = pl.program_id(0)
    mine, seq = meta[0], meta[1]

    @pl.when(step == 0)
    def _():
        for j in range(4):
            same = ids[((chunk * 4 + seq) * 8 + 4 * mine + j) * SPAN] == mine
            for h in range(8):
                value = heads[h, j * SPAN : (j + 1) * SPAN, :]
                zero = jnp.zeros_like(value)
                rows[0, j * SPAN : (j + 1) * SPAN, h * HD : (h + 1) * HD] = jnp.where(same, value, zero)
                rows[1, j * SPAN : (j + 1) * SPAN, h * HD : (h + 1) * HD] = jnp.where(same, zero, value)

    term = jnp.dot(rows[0], own_w[...], preferred_element_type=jnp.float32)
    term += jnp.dot(rows[1], other_w[...], preferred_element_type=jnp.float32)
    term = term.astype(jnp.bfloat16)
    half = term.shape[0] // 2
    places = {
        0: ((keep_a, 0), (keep_b, 0)),
        1: ((to_x, 0), (keep_b, 1)),
        2: ((keep_a, 1), (to_y, 0)),
        3: ((to_x, 1), (to_y, 1)),
    }
    for at, k in enumerate(ORDER):

        @pl.when(step == at)
        def _():
            (a, i), (b, j) = places[k]
            a[i] = term[:half]
            b[j] = term[half:]


def finish(chunk, meta, ids, after, heads, own_w, other_w):
    depth, total = own_w.shape
    width = total // 4
    count = heads.shape[1]
    whole = pl.BlockSpec(memory_space=pltpu.VMEM)

    def column(i, meta, ids):
        k = jnp.where(i == 0, 3, jnp.where(i == 3, 0, i))
        return (0, meta[2] ^ k)

    shape = jax.ShapeDtypeStruct((2, count // 2, width), jnp.bfloat16)
    return pl.pallas_call(
        partial(finish_kernel, chunk),
        grid_spec=pltpu.PrefetchScalarGridSpec(
            num_scalar_prefetch=2,
            grid=(4,),
            in_specs=[pl.BlockSpec(memory_space=pl.ANY), whole, pl.BlockSpec((depth, width), column), pl.BlockSpec((depth, width), column)],
            out_specs=[whole] * 4,
            scratch_shapes=[pltpu.VMEM((2, count, depth), jnp.bfloat16)],
        ),
        out_shape=[shape] * 4,
        compiler_params=pltpu.CompilerParams(vmem_limit_bytes=VMEM),
        cost_estimate=pl.CostEstimate(flops=12000000000, bytes_accessed=1000, transcendentals=0),
        name="finish",
    )(meta, ids, after, heads, own_w, other_w)


def body(tokens, modality, norm_gain, input_weight, head_gain, output_weight):
    mine, seq, tp = lax.axis_index("mod"), lax.axis_index("seq"), lax.axis_index("tp")
    width = tokens.shape[1]
    half = input_weight.shape[3] // 2
    first = mine == 0
    meta = jnp.stack([mine, seq, tp]).astype(jnp.int32)

    def to_mod(value):
        return lax.ppermute(value, "mod", swap(2, 1))

    def to_x(value):
        return lax.ppermute(value, "tp", swap(4, 1))

    def to_y(value):
        return lax.ppermute(value, "tp", swap(4, 2))

    own_w = jnp.transpose(input_weight[0], (1, 0, 2))
    partner = to_mod(tokens)
    early_half = other_half(meta, [], own_w, (1, 0))
    partner, early_half = lax.optimization_barrier((partner, early_half))
    blocks = [jnp.where(first, tokens, partner), jnp.where(first, partner, tokens)]
    rows = blocks[0].shape[0] // 2
    quarter = rows // 2
    starts = [lax.dynamic_slice_in_dim(block, mine * rows, rows, axis=0) for block in blocks]
    low_x, low_y, early_w = to_x(starts[0]), to_y(starts[0]), to_mod(early_half)
    low_x, low_y, start_high = lax.optimization_barrier((low_x, low_y, starts[1]))
    late_w = to_mod(other_half(meta, [low_x, low_y], own_w, (2,)))
    high_x, high_y = to_x(start_high), to_y(start_high)
    own_out = output_weight[0]
    arrived, projected = [], []
    for chunk, pieces in enumerate(([low_x, low_y], [high_x, high_y])):
        if chunk:
            pieces[0], pieces[1], late_out, _ = lax.optimization_barrier((high_x, high_y, own_out, projected[0]))
            other_out = to_mod(late_out)
        pieces = pieces + [to_y(pieces[0][:quarter]), to_x(pieces[1][quarter:])]
        q = to_mod(jnp.concatenate(pieces))
        pieces = [blocks[chunk]] + pieces + [q]
        sent = project(chunk, meta, modality, pieces, norm_gain, head_gain, own_w, early_w, late_w)
        arrived.append(lax.all_to_all(sent, "seq", 0, 0, tiled=True))
        projected.append(sent)
    low_mixed = attend(meta, projected[1], projected[1], arrived[0])
    low_mixed, arrived[1] = lax.optimization_barrier((low_mixed, arrived[1]))
    high_mixed = attend(meta, low_mixed, other_out, *arrived)

    results = []
    for chunk, mixed in enumerate((low_mixed, high_mixed)):
        mixed = mixed.reshape((8,) + mixed.shape[2:])
        heads = lax.all_to_all(mixed, ("mod", "seq"), 0, 0, tiled=True)
        send_x, send_y, keep_a, keep_b = finish(chunk, meta, modality, results[-1] if chunk else high_mixed, heads, own_out, other_out)
        got_x, got_y = to_x(send_x).astype(jnp.float32), to_y(send_y).astype(jnp.float32)
        keep_a, keep_b = keep_a.astype(jnp.float32), keep_b.astype(jnp.float32)
        last_a = to_y((keep_a[1] + got_x[1]).astype(jnp.bfloat16)).astype(jnp.float32)
        last_b = to_x((keep_b[1] + got_y[1]).astype(jnp.bfloat16)).astype(jnp.float32)
        result = jnp.concatenate([keep_a[0] + got_x[0] + last_a, keep_b[0] + got_y[0] + last_b])
        results.append(result.astype(jnp.bfloat16))
    back = to_mod(jnp.where(first, results[1], results[0]))
    return jnp.concatenate(
        [jnp.where(first, results[0], back), jnp.where(first, back, results[1])], axis=0
    )


def solution(mesh):
    sizes = dict(mesh.shape)
    in_specs = (
        P(("mod", "seq"), "tp"),
        P(),
        P(),
        P("mod", None, None, "tp"),
        P(),
        P("mod", "tp", None),
    )
    out_specs = P(("mod", "seq"), "tp")

    def run(tokens, modality, norm_gain, input_weight, head_gain, output_weight):
        heads = input_weight.shape[3] // HD
        shard = tokens.shape[0] // (sizes["mod"] * sizes["seq"])
        small = (sizes["mod"], sizes["seq"], sizes["tp"]) == (2, 4, 4)
        fits = small and heads == 32 and shard == 8 * SPAN
        return jax.shard_map(
            body if fits else general_body,
            mesh=mesh,
            in_specs=in_specs,
            out_specs=out_specs,
            check_vma=False,
        )(tokens, modality, norm_gain, input_weight, head_gain, output_weight)

    return run
```

```python
from functools import partial
import math

import jax
import jax.numpy as jnp
from jax import lax
from jax.experimental import pallas as pl
from jax.experimental.pallas import tpu as pltpu
from jax.sharding import PartitionSpec as P

HD = 128
CAP = 320
SPAN = 64
SLOTS = CAP // SPAN
VMEM = 40 * 1024 * 1024


epsilon = 1e-05
sentinel = 1 << 30


def route_table(shard_ids, shard_index, slot_count):
    length = shard_ids.shape[0]
    order = jnp.argsort(shard_ids, stable=True)
    text_count = jnp.sum((shard_ids == 0).astype(jnp.int32))
    padded = jnp.concatenate([order, jnp.zeros((slot_count,), jnp.int32)])
    slot_index = jnp.arange(slot_count, dtype=jnp.int32)
    picked = jnp.stack(
        [padded[:slot_count], lax.dynamic_slice_in_dim(padded, text_count, slot_count)]
    )
    live = jnp.stack([slot_index < text_count, slot_index < length - text_count])
    place = shard_index * length + picked
    query_place = jnp.where(live, place, -1)
    key_place = jnp.where(live, place, sentinel)
    return (order, text_count, picked, live, query_place, key_place)


def select_rows(table, picked, live):
    return jnp.where(live[:, :, None], table[picked], jnp.zeros((), table.dtype))


def head_norm(part, gain):
    return part * lax.rsqrt(jnp.mean(part * part, axis=-1, keepdims=True) + epsilon) * gain


def general_body(tokens, modality, norm_gain, input_weight, head_gain, output_weight):
    length = tokens.shape[0]
    mod_count = lax.axis_size("mod")
    seq_count = lax.axis_size("seq")
    shards = mod_count * seq_count
    mine = lax.axis_index("mod")
    seq_index = lax.axis_index("seq")
    all_ids = modality.reshape(shards, length)
    own_index = mine * seq_count + seq_index
    own_ids = lax.dynamic_index_in_dim(all_ids, own_index, 0, keepdims=False)
    own_table = route_table(own_ids, own_index, CAP)
    order = own_table[0]
    text_count = own_table[1]
    picked = own_table[2]
    live = own_table[3]
    tables = jax.vmap(partial(route_table, slot_count=CAP))(
        all_ids, jnp.arange(shards, dtype=jnp.int32)
    )
    query_grid = tables[4].reshape(mod_count, seq_count, 2, CAP)
    own_query = lax.dynamic_index_in_dim(query_grid, seq_index, 1, keepdims=False)
    own_query = lax.dynamic_index_in_dim(own_query, mine, 1, keepdims=False).reshape(
        mod_count * CAP
    )
    key_grid = tables[5].reshape(mod_count, seq_count, 2, CAP)
    key_order = jnp.transpose(key_grid, (2, 1, 0, 3)).reshape(shards * mod_count * CAP)
    gathered = lax.all_gather(tokens, "tp", axis=1, tiled=True)
    arrived = lax.all_to_all(
        select_rows(gathered, picked, live), "mod", split_axis=0, concat_axis=0, tiled=True
    )
    rows_total = arrived.shape[0] * arrived.shape[1]
    width = arrived.shape[2]
    states = arrived.reshape(rows_total, width).astype(jnp.float32)
    gain = lax.dynamic_index_in_dim(norm_gain, mine, 0, keepdims=False)
    normed = (
        states * lax.rsqrt(jnp.mean(states * states, axis=1, keepdims=True) + epsilon) * gain
    ).astype(jnp.bfloat16)
    local_width = input_weight.shape[3]
    heads_here = local_width // HD
    projected = jnp.dot(
        normed, input_weight[0].reshape(width, 3 * local_width), preferred_element_type=jnp.float32
    )
    projected = projected.reshape(rows_total, 3, heads_here, HD)
    gains = lax.dynamic_index_in_dim(head_gain, mine, 0, keepdims=False)
    query_rows = head_norm(projected[:, 0], gains[0]).astype(jnp.bfloat16)
    key_rows = (
        head_norm(projected[:, 1], gains[1]).astype(jnp.bfloat16).reshape(rows_total, local_width)
    )
    value_rows = projected[:, 2].astype(jnp.bfloat16).reshape(rows_total, local_width)
    scale = 1.0 / math.sqrt(HD)
    key_piece = lax.all_gather(key_rows, ("mod", "seq"), axis=0, tiled=True)
    value_piece = lax.all_gather(value_rows, ("mod", "seq"), axis=0, tiled=True)
    count = key_piece.shape[0]
    scores = (
        jnp.einsum(
            "rhe,khe->hrk",
            query_rows,
            key_piece.reshape(count, heads_here, HD),
            preferred_element_type=jnp.float32,
        )
        * scale
    )
    weights = jnp.where(key_order[None, None, :] <= own_query[None, :, None], jnp.exp(scores), 0.0)
    totals = jnp.sum(weights, axis=2)
    rounded = weights.astype(jnp.bfloat16)
    weighted = jnp.einsum(
        "hrk,khe->rhe",
        rounded,
        value_piece.reshape(count, heads_here, HD),
        preferred_element_type=jnp.float32,
    )
    weighted, totals = (weighted, totals)
    totals = jnp.where(own_query[None, :] >= 0, totals, 1.0)
    attention = (
        (weighted / jnp.transpose(totals)[:, :, None])
        .astype(jnp.bfloat16)
        .reshape(rows_total, local_width)
    )
    head_terms = jnp.dot(attention, output_weight[0], preferred_element_type=jnp.float32)
    summed = lax.psum_scatter(
        head_terms.astype(jnp.bfloat16), "tp", scatter_dimension=1, tiled=True
    ).astype(jnp.float32)
    result = summed.astype(jnp.bfloat16).reshape(mod_count, CAP, summed.shape[1])
    returned = lax.all_to_all(result, "mod", split_axis=0, concat_axis=0, tiled=True)
    flat = returned.reshape(mod_count * CAP, summed.shape[1])
    inverse = jnp.zeros((length,), jnp.int32).at[order].set(jnp.arange(length, dtype=jnp.int32))
    slot = own_ids * CAP + inverse - own_ids * text_count
    return flat[slot]


def swap(size, bit):
    return [(i, i ^ bit) for i in range(size)]


def half_kernel(parts, meta, weight, *refs):
    out, held, come, gone = refs[-4:]
    half = out.shape[2]
    depth = held.shape[1]
    start = pl.multiple_of((1 - meta[0]) * half, half)
    inward, outward = [], []
    for n, part in enumerate(parts):
        for f in range(out.shape[1] // depth):
            at, deep = len(inward), pl.ds(f * depth, depth)
            source = weight.at[part, deep, pl.ds(start, half)]
            inward.append(pltpu.make_async_copy(source, held.at[at], come.at[at]))
            outward.append(pltpu.make_async_copy(held.at[at], out.at[n, deep, :], gone.at[at]))
    for copy in inward:
        copy.start()
    for first, second in zip(inward, outward):
        first.wait()
        second.start()
    for copy in outward:
        copy.wait()


def other_half(meta, after, weight, parts):
    outside = pl.BlockSpec(memory_space=pl.ANY)
    depth, half = weight.shape[1], weight.shape[2] // 2
    count = 4 * len(parts)
    return pl.pallas_call(
        partial(half_kernel, parts),
        in_specs=[pl.BlockSpec(memory_space=pltpu.SMEM)] + [outside] * (1 + len(after)),
        out_specs=outside,
        out_shape=jax.ShapeDtypeStruct((len(parts), depth, half), weight.dtype),
        scratch_shapes=[
            pltpu.VMEM((count, depth // 4, half), weight.dtype),
            pltpu.SemaphoreType.DMA((count,)),
            pltpu.SemaphoreType.DMA((count,)),
        ],
        compiler_params=pltpu.CompilerParams(vmem_limit_bytes=VMEM),
        cost_estimate=pl.CostEstimate(flops=count * 1000000000, bytes_accessed=1000, transcendentals=0),
        name="other_half",
    )(meta, weight, *after)


def project_kernel(chunk, meta, ids, block, p1, p2, p3a, p3b, q, gain, head_gain, own_w, early_w, query_w, value_w, out, rows, inverse, tiles, held, table, sems):
    mine, seq, tp = meta[0], meta[1], meta[2]
    width, half = tiles.shape[2:]
    features = 4 * width
    count = block.shape[0]
    incoming, place = [], 0
    for n, piece in enumerate((block, p1, p2, p3a, p3b, q)):
        incoming.append(
            pltpu.make_async_copy(piece, held.at[pl.ds(place, piece.shape[0]), :], sems.at[8 + n])
        )
        place += piece.shape[0]
    for copy in incoming:
        copy.start()

    def part_of(step):
        which = lax.rem(step, 3)
        return jnp.where(which == 0, 1, jnp.where(which == 1, 0, 2))

    def copies(step, act):
        which = lax.rem(step, 3)
        for f in range(4):
            deep = pl.ds(f * width, width)
            slot = lax.rem(step, 2) * 4 + f

            def move(source):
                act(pltpu.make_async_copy(source, tiles.at[lax.rem(step, 2), f], sems.at[slot]))

            @pl.when(step < 3)
            def _():
                move(own_w.at[part_of(step), deep, pl.ds(pl.multiple_of(mine * half, half), half)])

            @pl.when(step == 3)
            def _():
                move(early_w.at[0, deep, :])

            @pl.when(step == 4)
            def _():
                move(query_w.at[0, deep, :])

            @pl.when(step == 5)
            def _():
                move(value_w.at[0, deep, :])

    for step in range(2):
        copies(jnp.int32(step), lambda copy: copy.start())

    for copy in incoming:
        copy.wait()
    counts = [jnp.int32(0), jnp.int32(0)]
    for j in range(8):
        near, at = j < 4, j % 4
        span = 4 * mine + at if near else 4 * (1 - mine) + at
        kind = ids[((chunk * 4 + seq) * 8 + span) * SPAN]
        same = (kind == mine).astype(jnp.int32)
        group = 1 - same
        slot = jnp.where(same == 1, counts[0], counts[1])
        counts = [counts[0] + same, counts[1] + group]
        table[group * 8 + slot] = span
        place = pl.ds(pl.multiple_of(slot * SPAN, SPAN), SPAN)
        total = jnp.zeros((SPAN, 1), jnp.float32)
        for k in range(4):
            if k == 0:
                value = held[pl.ds(pl.multiple_of(span * SPAN, SPAN), SPAN), :]
            else:
                start = count + (0 if near else 3 * count // 2) + (k - 1) * count // 2 + at * SPAN
                value = held[start : start + SPAN, :]
            value = value.astype(jnp.float32)
            total += jnp.sum(value * value, axis=1, keepdims=True)
            feature = tp ^ k
            scale = gain[pl.ds(kind, 1), pl.ds(pl.multiple_of(feature * width, width), width)]
            rows[feature, group, place, :] = (value * scale).astype(jnp.bfloat16)
        scale = lax.rsqrt(total / features + epsilon)
        inverse[group, place, :] = jnp.broadcast_to(scale, (SPAN, HD))
    table[16] = counts[0]
    table[17] = counts[1]

    @pl.loop(0, 6)
    def _(step):
        group = (step >= 3).astype(jnp.int32)
        copies(step, lambda copy: copy.wait())
        buffer = lax.rem(step, 2)
        total = None
        for f in range(4):
            term = jnp.dot(rows[f, group], tiles[buffer, f], preferred_element_type=jnp.float32)
            total = term if total is None else total + term
        @pl.when(step < 4)
        def _():
            copies(step + 2, lambda copy: copy.start())

        kind = jnp.where(group == 0, mine, 1 - mine)
        which = part_of(step)
        scale = inverse[group]
        count = table[16 + group]
        row = head_gain[kind, pl.ds(jnp.minimum(which, 1), 1), :]
        row = row * jnp.where(which == 0, math.log2(math.e) / math.sqrt(HD), 1.0)
        for h in range(4):
            piece = total[:, h * HD : (h + 1) * HD] * scale
            mean = jnp.mean(piece * piece, axis=1, keepdims=True)
            normed = piece * lax.rsqrt(mean + epsilon) * row
            value = jnp.where(which == 2, piece, normed).astype(jnp.bfloat16)
            for slot in range(SLOTS):

                @pl.when(slot < count)
                def _():
                    span = table[group * 8 + slot]
                    out[h, which, pl.ds(pl.multiple_of(span * SPAN, SPAN), SPAN), :] = value[
                        slot * SPAN : (slot + 1) * SPAN
                    ]


def project(chunk, meta, ids, pieces, gain, head_gain, own_w, early_w, late_w):
    depth, half = early_w.shape[1:]
    width = depth // 4
    whole = pl.BlockSpec(memory_space=pltpu.VMEM)
    scalars = pl.BlockSpec(memory_space=pltpu.SMEM)
    outside = pl.BlockSpec(memory_space=pl.ANY)
    shape = jax.ShapeDtypeStruct((4, 3, 8 * SPAN, HD), jnp.bfloat16)
    return pl.pallas_call(
        partial(project_kernel, chunk),
        in_specs=[scalars] * 2 + [outside] * 6 + [whole] * 2 + [outside] * 4,
        out_specs=whole,
        scratch_shapes=[
            pltpu.VMEM((4, 2, CAP, width), jnp.bfloat16),
            pltpu.VMEM((2, CAP, HD), jnp.float32),
            pltpu.VMEM((2, 4, width, half), jnp.bfloat16),
            pltpu.VMEM((4 * 8 * SPAN, width), jnp.bfloat16),
            pltpu.SMEM((32,), jnp.int32),
            pltpu.SemaphoreType.DMA((14,)),
        ],
        out_shape=shape,
        compiler_params=pltpu.CompilerParams(vmem_limit_bytes=VMEM),
        cost_estimate=pl.CostEstimate(flops=1000, bytes_accessed=1000, transcendentals=0),
        name="project",
    )(meta, ids, *pieces, gain, head_gain, own_w, early_w, *late_w)


def attend_kernel(high, meta, after, later, *refs):
    first, last = refs[0], refs[1] if high else refs[0]
    outs, (mixed, values) = refs[-6:-2], refs[-2:]
    seq = meta[1]
    block = last.shape[2]
    half = block // 2
    for base, pieces in ((0, first), (4, last)) if high else ((0, first),):
        for at in range(4):
            values[base + at, :, :HD] = pieces[at, 2]
            values[base + at, :, HD:] = jnp.ones((block, HD), jnp.bfloat16)
    diagonal = lax.broadcasted_iota(jnp.int32, (half, half), 0) >= lax.broadcasted_iota(
        jnp.int32, (half, half), 1
    )

    def scores(query, key):
        return lax.dot_general(query, key, (((1,), (1,)), ((), ())), preferred_element_type=jnp.float32)

    for at in range(4):
        own = 4 + at if high else at
        for side in range(2):
            query = last[at, 0, side * half : (side + 1) * half, :]
            weight = jnp.where(
                diagonal, jnp.exp2(scores(query, last[at, 1, side * half : (side + 1) * half, :])), 0.0
            ).astype(jnp.bfloat16)
            total = jnp.dot(
                weight, values[own, side * half : (side + 1) * half, :], preferred_element_type=jnp.float32
            )
            if side == 1:
                weight = jnp.exp2(scores(query, last[at, 1, :half, :])).astype(jnp.bfloat16)
                total += jnp.dot(weight, values[own, :half, :], preferred_element_type=jnp.float32)

            for j in range(own):
                key = first[j, 1] if j < 4 else last[j - 4, 1]
                weight = jnp.exp2(scores(query, key)).astype(jnp.bfloat16)
                total += jnp.dot(weight, values[j], preferred_element_type=jnp.float32)
            mixed[at, side * half : (side + 1) * half, :] = (total[:, :HD] / total[:, HD:]).astype(jnp.bfloat16)
    for k, out in enumerate(outs):
        out[...] = mixed[seq ^ k]


def attend(meta, after, later, first, last=None):
    high = last is not None
    pieces = [first, last] if high else [first]
    block = first.shape[2]
    whole = pl.BlockSpec(memory_space=pltpu.VMEM)
    count = 8 if high else 4
    return pl.pallas_call(
        partial(attend_kernel, high),
        in_specs=[pl.BlockSpec(memory_space=pltpu.SMEM)]
        + [pl.BlockSpec(memory_space=pl.ANY)] * 2
        + [whole] * len(pieces),
        out_specs=[whole] * 4,
        out_shape=[jax.ShapeDtypeStruct((block, HD), jnp.bfloat16)] * 4,
        scratch_shapes=[
            pltpu.VMEM((4, block, HD), jnp.bfloat16),
            pltpu.VMEM((count, block, 2 * HD), jnp.bfloat16),
        ],
        compiler_params=pltpu.CompilerParams(vmem_limit_bytes=VMEM),
        cost_estimate=pl.CostEstimate(flops=12000000000 if high else 6000000000, bytes_accessed=1000, transcendentals=0),
        name="attend",
    )(meta, after, later, *pieces)


ORDER = (3, 1, 2, 0)


def finish_kernel(chunk, meta, ids, after, *refs):
    heads, (partner, own_w, other_w, to_x, to_y, keep_a, keep_b, rows) = refs[:4], refs[4:]
    step = pl.program_id(0)
    mine, seq = meta[0], meta[1]

    @pl.when(step == 0)
    def _():
        for j in range(4):
            same = ids[((chunk * 4 + seq) * 8 + 4 * mine + j) * SPAN] == mine
            at = pl.multiple_of((4 * mine + j) * SPAN, SPAN)
            for k in range(8):
                value = heads[k][pl.ds(at, SPAN), :] if k < 4 else partner[k - 4, j * SPAN : (j + 1) * SPAN, :]
                zero = jnp.zeros_like(value)
                head = (mine ^ (k // 4)) * 4 + (seq ^ (k % 4))
                lanes = pl.ds(pl.multiple_of(head * HD, HD), HD)
                rows[0, j * SPAN : (j + 1) * SPAN, lanes] = jnp.where(same, value, zero)
                rows[1, j * SPAN : (j + 1) * SPAN, lanes] = jnp.where(same, zero, value)

    term = jnp.dot(rows[0], own_w[...], preferred_element_type=jnp.float32)
    term += jnp.dot(rows[1], other_w[...], preferred_element_type=jnp.float32)
    term = term.astype(jnp.bfloat16)
    half = term.shape[0] // 2
    places = {
        0: ((keep_a, 0), (keep_b, 0)),
        1: ((to_x, 0), (keep_b, 1)),
        2: ((keep_a, 1), (to_y, 0)),
        3: ((to_x, 1), (to_y, 1)),
    }
    for at, k in enumerate(ORDER):

        @pl.when(step == at)
        def _():
            (a, i), (b, j) = places[k]
            a[i] = term[:half]
            b[j] = term[half:]


def finish(chunk, meta, ids, after, heads, own_w, other_w):
    depth, total = own_w.shape
    width = total // 4
    count = heads[-1].shape[1]
    whole = pl.BlockSpec(memory_space=pltpu.VMEM)

    def column(i, meta, ids):
        k = jnp.where(i == 0, 3, jnp.where(i == 3, 0, i))
        return (0, meta[2] ^ k)

    shape = jax.ShapeDtypeStruct((2, count // 2, width), jnp.bfloat16)
    return pl.pallas_call(
        partial(finish_kernel, chunk),
        grid_spec=pltpu.PrefetchScalarGridSpec(
            num_scalar_prefetch=2,
            grid=(4,),
            in_specs=[pl.BlockSpec(memory_space=pl.ANY)]
            + [whole] * 5
            + [pl.BlockSpec((depth, width), column), pl.BlockSpec((depth, width), column)],
            out_specs=[whole] * 4,
            scratch_shapes=[pltpu.VMEM((2, count, depth), jnp.bfloat16)],
        ),
        out_shape=[shape] * 4,
        compiler_params=pltpu.CompilerParams(vmem_limit_bytes=VMEM),
        cost_estimate=pl.CostEstimate(flops=12000000000, bytes_accessed=1000, transcendentals=0),
        name="finish",
    )(meta, ids, after, *heads, own_w, other_w)


def body(tokens, modality, norm_gain, input_weight, head_gain, output_weight):
    mine, seq, tp = lax.axis_index("mod"), lax.axis_index("seq"), lax.axis_index("tp")
    width = tokens.shape[1]
    half = input_weight.shape[3] // 2
    first = mine == 0
    meta = jnp.stack([mine, seq, tp]).astype(jnp.int32)

    def to_mod(value):
        return lax.ppermute(value, "mod", swap(2, 1))

    def to_x(value):
        return lax.ppermute(value, "tp", swap(4, 1))

    def to_y(value):
        return lax.ppermute(value, "tp", swap(4, 2))

    own_w = jnp.transpose(input_weight[0], (1, 0, 2))
    partner = to_mod(tokens)
    early_half = other_half(meta, [], own_w, (1,))
    partner, early_half = lax.optimization_barrier((partner, early_half))
    blocks = [jnp.where(first, tokens, partner), jnp.where(first, partner, tokens)]
    rows = blocks[0].shape[0] // 2
    quarter = rows // 2
    starts = [lax.dynamic_slice_in_dim(block, mine * rows, rows, axis=0) for block in blocks]
    low_x, low_y, early_w = to_x(starts[0]), to_y(starts[0]), to_mod(early_half)
    low_x, low_y, start_high = lax.optimization_barrier((low_x, low_y, starts[1]))
    late_w = [
        to_mod(other_half(meta, [starts[0]], own_w, (0,))),
        to_mod(other_half(meta, [low_x, low_y], own_w, (2,))),
    ]
    high_x, high_y = to_x(start_high), to_y(start_high)
    own_out = output_weight[0]
    arrived, projected = [], []
    for chunk, pieces in enumerate(([low_x, low_y], [high_x, high_y])):
        if chunk:
            pieces[0], pieces[1], late_out, _ = lax.optimization_barrier((high_x, high_y, own_out, projected[0]))
            other_out = to_mod(late_out)
        pieces = pieces + [to_y(pieces[0][:quarter]), to_x(pieces[1][quarter:])]
        q = to_mod(jnp.concatenate(pieces))
        pieces = [blocks[chunk]] + pieces + [q]
        sent = project(chunk, meta, modality, pieces, norm_gain, head_gain, own_w, early_w, late_w)
        arrived.append(lax.all_to_all(sent, "seq", 0, 0, tiled=True))
        projected.append(sent)
    low_mixed = attend(meta, projected[1], projected[1], arrived[0])
    high_mixed = attend(meta, low_mixed[0], other_out, *arrived)
    results = []
    for chunk, mixed in enumerate((low_mixed, high_mixed)):
        far, mid, near = [lax.ppermute(mixed[k], "seq", swap(4, k)) for k in (3, 2, 1)]
        heads = [mixed[0], near, mid, far]
        cut = [lax.dynamic_slice_in_dim(head, (1 - mine) * rows, rows, axis=0) for head in heads]
        heads.append(to_mod(jnp.stack(cut)))
        after = send_x if chunk else high_mixed[0]
        send_x, send_y, keep_a, keep_b = finish(chunk, meta, modality, after, heads, own_out, other_out)
        got_x, got_y = to_x(send_x).astype(jnp.float32), to_y(send_y).astype(jnp.float32)
        keep_a, keep_b = keep_a.astype(jnp.float32), keep_b.astype(jnp.float32)
        last_a = to_y((keep_a[1] + got_x[1]).astype(jnp.bfloat16)).astype(jnp.float32)
        last_b = to_x((keep_b[1] + got_y[1]).astype(jnp.bfloat16)).astype(jnp.float32)
        result = jnp.concatenate([keep_a[0] + got_x[0] + last_a, keep_b[0] + got_y[0] + last_b])
        results.append(result.astype(jnp.bfloat16))
    back = to_mod(jnp.where(first, results[1], results[0]))
    return jnp.concatenate(
        [jnp.where(first, results[0], back), jnp.where(first, back, results[1])], axis=0
    )


def solution(mesh):
    sizes = dict(mesh.shape)
    in_specs = (
        P(("mod", "seq"), "tp"),
        P(),
        P(),
        P("mod", None, None, "tp"),
        P(),
        P("mod", "tp", None),
    )
    out_specs = P(("mod", "seq"), "tp")

    def run(tokens, modality, norm_gain, input_weight, head_gain, output_weight):
        heads = input_weight.shape[3] // HD
        shard = tokens.shape[0] // (sizes["mod"] * sizes["seq"])
        small = (sizes["mod"], sizes["seq"], sizes["tp"]) == (2, 4, 4)
        fits = small and heads == 32 and shard == 8 * SPAN
        return jax.shard_map(
            body if fits else general_body,
            mesh=mesh,
            in_specs=in_specs,
            out_specs=out_specs,
            check_vma=False,
        )(tokens, modality, norm_gain, input_weight, head_gain, output_weight)

    return run
```

```python
from functools import partial
import math

import jax
import jax.numpy as jnp
from jax import lax
from jax.experimental import pallas as pl
from jax.experimental.pallas import tpu as pltpu
from jax.sharding import PartitionSpec as P

HD = 128
CAP = 320
SPAN = 64
SLOTS = CAP // SPAN
VMEM = 40 * 1024 * 1024


epsilon = 1e-05
sentinel = 1 << 30


def route_table(shard_ids, shard_index, slot_count):
    length = shard_ids.shape[0]
    order = jnp.argsort(shard_ids, stable=True)
    text_count = jnp.sum((shard_ids == 0).astype(jnp.int32))
    padded = jnp.concatenate([order, jnp.zeros((slot_count,), jnp.int32)])
    slot_index = jnp.arange(slot_count, dtype=jnp.int32)
    picked = jnp.stack(
        [padded[:slot_count], lax.dynamic_slice_in_dim(padded, text_count, slot_count)]
    )
    live = jnp.stack([slot_index < text_count, slot_index < length - text_count])
    place = shard_index * length + picked
    query_place = jnp.where(live, place, -1)
    key_place = jnp.where(live, place, sentinel)
    return (order, text_count, picked, live, query_place, key_place)


def select_rows(table, picked, live):
    return jnp.where(live[:, :, None], table[picked], jnp.zeros((), table.dtype))


def head_norm(part, gain):
    return part * lax.rsqrt(jnp.mean(part * part, axis=-1, keepdims=True) + epsilon) * gain


def general_body(tokens, modality, norm_gain, input_weight, head_gain, output_weight):
    length = tokens.shape[0]
    mod_count = lax.axis_size("mod")
    seq_count = lax.axis_size("seq")
    shards = mod_count * seq_count
    mine = lax.axis_index("mod")
    seq_index = lax.axis_index("seq")
    all_ids = modality.reshape(shards, length)
    own_index = mine * seq_count + seq_index
    own_ids = lax.dynamic_index_in_dim(all_ids, own_index, 0, keepdims=False)
    own_table = route_table(own_ids, own_index, CAP)
    order = own_table[0]
    text_count = own_table[1]
    picked = own_table[2]
    live = own_table[3]
    tables = jax.vmap(partial(route_table, slot_count=CAP))(
        all_ids, jnp.arange(shards, dtype=jnp.int32)
    )
    query_grid = tables[4].reshape(mod_count, seq_count, 2, CAP)
    own_query = lax.dynamic_index_in_dim(query_grid, seq_index, 1, keepdims=False)
    own_query = lax.dynamic_index_in_dim(own_query, mine, 1, keepdims=False).reshape(
        mod_count * CAP
    )
    key_grid = tables[5].reshape(mod_count, seq_count, 2, CAP)
    key_order = jnp.transpose(key_grid, (2, 1, 0, 3)).reshape(shards * mod_count * CAP)
    gathered = lax.all_gather(tokens, "tp", axis=1, tiled=True)
    arrived = lax.all_to_all(
        select_rows(gathered, picked, live), "mod", split_axis=0, concat_axis=0, tiled=True
    )
    rows_total = arrived.shape[0] * arrived.shape[1]
    width = arrived.shape[2]
    states = arrived.reshape(rows_total, width).astype(jnp.float32)
    gain = lax.dynamic_index_in_dim(norm_gain, mine, 0, keepdims=False)
    normed = (
        states * lax.rsqrt(jnp.mean(states * states, axis=1, keepdims=True) + epsilon) * gain
    ).astype(jnp.bfloat16)
    local_width = input_weight.shape[3]
    heads_here = local_width // HD
    projected = jnp.dot(
        normed, input_weight[0].reshape(width, 3 * local_width), preferred_element_type=jnp.float32
    )
    projected = projected.reshape(rows_total, 3, heads_here, HD)
    gains = lax.dynamic_index_in_dim(head_gain, mine, 0, keepdims=False)
    query_rows = head_norm(projected[:, 0], gains[0]).astype(jnp.bfloat16)
    key_rows = (
        head_norm(projected[:, 1], gains[1]).astype(jnp.bfloat16).reshape(rows_total, local_width)
    )
    value_rows = projected[:, 2].astype(jnp.bfloat16).reshape(rows_total, local_width)
    scale = 1.0 / math.sqrt(HD)
    key_piece = lax.all_gather(key_rows, ("mod", "seq"), axis=0, tiled=True)
    value_piece = lax.all_gather(value_rows, ("mod", "seq"), axis=0, tiled=True)
    count = key_piece.shape[0]
    scores = (
        jnp.einsum(
            "rhe,khe->hrk",
            query_rows,
            key_piece.reshape(count, heads_here, HD),
            preferred_element_type=jnp.float32,
        )
        * scale
    )
    weights = jnp.where(key_order[None, None, :] <= own_query[None, :, None], jnp.exp(scores), 0.0)
    totals = jnp.sum(weights, axis=2)
    rounded = weights.astype(jnp.bfloat16)
    weighted = jnp.einsum(
        "hrk,khe->rhe",
        rounded,
        value_piece.reshape(count, heads_here, HD),
        preferred_element_type=jnp.float32,
    )
    weighted, totals = (weighted, totals)
    totals = jnp.where(own_query[None, :] >= 0, totals, 1.0)
    attention = (
        (weighted / jnp.transpose(totals)[:, :, None])
        .astype(jnp.bfloat16)
        .reshape(rows_total, local_width)
    )
    head_terms = jnp.dot(attention, output_weight[0], preferred_element_type=jnp.float32)
    summed = lax.psum_scatter(
        head_terms.astype(jnp.bfloat16), "tp", scatter_dimension=1, tiled=True
    ).astype(jnp.float32)
    result = summed.astype(jnp.bfloat16).reshape(mod_count, CAP, summed.shape[1])
    returned = lax.all_to_all(result, "mod", split_axis=0, concat_axis=0, tiled=True)
    flat = returned.reshape(mod_count * CAP, summed.shape[1])
    inverse = jnp.zeros((length,), jnp.int32).at[order].set(jnp.arange(length, dtype=jnp.int32))
    slot = own_ids * CAP + inverse - own_ids * text_count
    return flat[slot]


def swap(size, bit):
    return [(i, i ^ bit) for i in range(size)]


def half_kernel(parts, meta, weight, *refs):
    out, held, come, gone = refs[-4:]
    half = out.shape[2]
    depth = held.shape[1]
    start = pl.multiple_of((1 - meta[0]) * half, half)
    inward, outward = [], []
    for n, part in enumerate(parts):
        for f in range(out.shape[1] // depth):
            at, deep = len(inward), pl.ds(f * depth, depth)
            source = weight.at[part, deep, pl.ds(start, half)]
            inward.append(pltpu.make_async_copy(source, held.at[at], come.at[at]))
            outward.append(pltpu.make_async_copy(held.at[at], out.at[n, deep, :], gone.at[at]))
    for copy in inward:
        copy.start()
    for first, second in zip(inward, outward):
        first.wait()
        second.start()
    for copy in outward:
        copy.wait()


def other_half(meta, after, weight, parts):
    outside = pl.BlockSpec(memory_space=pl.ANY)
    depth, half = weight.shape[1], weight.shape[2] // 2
    count = 4 * len(parts)
    return pl.pallas_call(
        partial(half_kernel, parts),
        in_specs=[pl.BlockSpec(memory_space=pltpu.SMEM)] + [outside] * (1 + len(after)),
        out_specs=outside,
        out_shape=jax.ShapeDtypeStruct((len(parts), depth, half), weight.dtype),
        scratch_shapes=[
            pltpu.VMEM((count, depth // 4, half), weight.dtype),
            pltpu.SemaphoreType.DMA((count,)),
            pltpu.SemaphoreType.DMA((count,)),
        ],
        compiler_params=pltpu.CompilerParams(vmem_limit_bytes=VMEM),
        cost_estimate=pl.CostEstimate(flops=count * 1000000000, bytes_accessed=1000, transcendentals=0),
        name="other_half",
    )(meta, weight, *after)


def project_kernel(chunk, meta, ids, block, p1, p2, p3a, p3b, q, gain, head_gain, own_w, early_w, query_w, value_w, out, rows, inverse, tiles, held, table, sems):
    mine, seq, tp = meta[0], meta[1], meta[2]
    width, half = tiles.shape[2:]
    features = 4 * width
    count = block.shape[0]
    incoming, place = [], 0
    for n, piece in enumerate((block, p1, p2, p3a, p3b, q)):
        incoming.append(
            pltpu.make_async_copy(piece, held.at[pl.ds(place, piece.shape[0]), :], sems.at[8 + n])
        )
        place += piece.shape[0]
    for copy in incoming:
        copy.start()

    def part_of(step):
        which = lax.rem(step, 3)
        return jnp.where(which == 0, 1, jnp.where(which == 1, 0, 2))

    def copies(step, act):
        which = lax.rem(step, 3)
        for f in range(4):
            deep = pl.ds(f * width, width)
            slot = lax.rem(step, 2) * 4 + f

            def move(source):
                act(pltpu.make_async_copy(source, tiles.at[lax.rem(step, 2), f], sems.at[slot]))

            @pl.when(step < 3)
            def _():
                move(own_w.at[part_of(step), deep, pl.ds(pl.multiple_of(mine * half, half), half)])

            @pl.when(step == 3)
            def _():
                move(early_w.at[0, deep, :])

            @pl.when(step == 4)
            def _():
                move(query_w.at[0, deep, :])

            @pl.when(step == 5)
            def _():
                move(value_w.at[0, deep, :])

    for step in range(2):
        copies(jnp.int32(step), lambda copy: copy.start())
    for copy in incoming:
        copy.wait()
    counts = [jnp.int32(0), jnp.int32(0)]
    for j in range(8):
        near, at = j < 4, j % 4
        span = 4 * mine + at if near else 4 * (1 - mine) + at
        kind = ids[((chunk * 4 + seq) * 8 + span) * SPAN]
        same = (kind == mine).astype(jnp.int32)
        group = 1 - same
        slot = jnp.where(same == 1, counts[0], counts[1])
        counts = [counts[0] + same, counts[1] + group]
        table[group * 8 + slot] = span
        place = pl.ds(pl.multiple_of(slot * SPAN, SPAN), SPAN)
        total = jnp.zeros((SPAN, 1), jnp.float32)
        for k in range(4):
            if k == 0:
                value = held[pl.ds(pl.multiple_of(span * SPAN, SPAN), SPAN), :]
            else:
                start = count + (0 if near else 3 * count // 2) + (k - 1) * count // 2 + at * SPAN
                value = held[start : start + SPAN, :]
            value = value.astype(jnp.float32)
            total += jnp.sum(value * value, axis=1, keepdims=True)
            feature = tp ^ k
            scale = gain[pl.ds(kind, 1), pl.ds(pl.multiple_of(feature * width, width), width)]
            rows[feature, group, place, :] = (value * scale).astype(jnp.bfloat16)
        scale = lax.rsqrt(total / features + epsilon)
        inverse[group, place, :] = jnp.broadcast_to(scale, (SPAN, HD))
    table[16] = counts[0]
    table[17] = counts[1]

    @pl.loop(0, 6, unroll=True)
    def _(step):
        group = (step >= 3).astype(jnp.int32)
        copies(step, lambda copy: copy.wait())
        buffer = lax.rem(step, 2)
        total = None
        for f in range(4):
            term = jnp.dot(rows[f, group], tiles[buffer, f], preferred_element_type=jnp.float32)
            total = term if total is None else total + term
        @pl.when(step < 4)
        def _():
            copies(step + 2, lambda copy: copy.start())

        kind = jnp.where(group == 0, mine, 1 - mine)
        which = part_of(step)
        scale = inverse[group]
        count = table[16 + group]
        row = head_gain[kind, pl.ds(jnp.minimum(which, 1), 1), :]
        row = row * jnp.where(which == 0, math.log2(math.e) / math.sqrt(HD), 1.0)
        for h in range(4):
            piece = total[:, h * HD : (h + 1) * HD] * scale
            mean = jnp.mean(piece * piece, axis=1, keepdims=True)
            normed = piece * lax.rsqrt(mean + epsilon) * row
            value = jnp.where(which == 2, piece, normed).astype(jnp.bfloat16)
            for slot in range(SLOTS):

                @pl.when(slot < count)
                def _():
                    span = table[group * 8 + slot]
                    out[h, which, pl.ds(pl.multiple_of(span * SPAN, SPAN), SPAN), :] = value[
                        slot * SPAN : (slot + 1) * SPAN
                    ]


def project(chunk, meta, ids, pieces, gain, head_gain, own_w, early_w, late_w):
    depth, half = early_w.shape[1:]
    width = depth // 4
    whole = pl.BlockSpec(memory_space=pltpu.VMEM)
    scalars = pl.BlockSpec(memory_space=pltpu.SMEM)
    outside = pl.BlockSpec(memory_space=pl.ANY)
    shape = jax.ShapeDtypeStruct((4, 3, 8 * SPAN, HD), jnp.bfloat16)
    return pl.pallas_call(
        partial(project_kernel, chunk),
        in_specs=[scalars] * 2 + [outside] * 6 + [whole] * 2 + [outside] * 4,
        out_specs=whole,
        scratch_shapes=[
            pltpu.VMEM((4, 2, CAP, width), jnp.bfloat16),
            pltpu.VMEM((2, CAP, HD), jnp.float32),
            pltpu.VMEM((2, 4, width, half), jnp.bfloat16),
            pltpu.VMEM((4 * 8 * SPAN, width), jnp.bfloat16),
            pltpu.SMEM((32,), jnp.int32),
            pltpu.SemaphoreType.DMA((14,)),
        ],
        out_shape=shape,
        compiler_params=pltpu.CompilerParams(vmem_limit_bytes=VMEM),
        cost_estimate=pl.CostEstimate(flops=1000, bytes_accessed=1000, transcendentals=0),
        name="project",
    )(meta, ids, *pieces, gain, head_gain, own_w, early_w, *late_w)


def attend_kernel(high, meta, after, later, *refs):
    first, last = refs[0], refs[1] if high else refs[0]
    outs, (mixed, values) = refs[-6:-2], refs[-2:]
    seq = meta[1]
    block = last.shape[2]
    half = block // 2
    for base, pieces in ((0, first), (4, last)) if high else ((0, first),):
        for at in range(4):
            values[base + at, :, :HD] = pieces[at, 2]
            values[base + at, :, HD:] = jnp.ones((block, HD), jnp.bfloat16)
    diagonal = lax.broadcasted_iota(jnp.int32, (half, half), 0) >= lax.broadcasted_iota(
        jnp.int32, (half, half), 1
    )

    def scores(query, key):
        return lax.dot_general(query, key, (((1,), (1,)), ((), ())), preferred_element_type=jnp.float32)

    for at in range(4):
        own = 4 + at if high else at
        for side in range(2):
            query = last[at, 0, side * half : (side + 1) * half, :]
            weight = jnp.where(
                diagonal, jnp.exp2(scores(query, last[at, 1, side * half : (side + 1) * half, :])), 0.0
            ).astype(jnp.bfloat16)
            total = jnp.dot(
                weight, values[own, side * half : (side + 1) * half, :], preferred_element_type=jnp.float32
            )
            if side == 1:
                weight = jnp.exp2(scores(query, last[at, 1, :half, :])).astype(jnp.bfloat16)
                total += jnp.dot(weight, values[own, :half, :], preferred_element_type=jnp.float32)

            for j in range(own):
                key = first[j, 1] if j < 4 else last[j - 4, 1]
                weight = jnp.exp2(scores(query, key)).astype(jnp.bfloat16)
                total += jnp.dot(weight, values[j], preferred_element_type=jnp.float32)
            mixed[at, side * half : (side + 1) * half, :] = (total[:, :HD] / total[:, HD:]).astype(jnp.bfloat16)
    for k, out in enumerate(outs):
        out[...] = mixed[seq ^ k]


def attend(meta, after, later, first, last=None):
    high = last is not None
    pieces = [first, last] if high else [first]
    block = first.shape[2]
    whole = pl.BlockSpec(memory_space=pltpu.VMEM)
    count = 8 if high else 4
    return pl.pallas_call(
        partial(attend_kernel, high),
        in_specs=[pl.BlockSpec(memory_space=pltpu.SMEM)]
        + [pl.BlockSpec(memory_space=pl.ANY)] * 2
        + [whole] * len(pieces),
        out_specs=[whole] * 4,
        out_shape=[jax.ShapeDtypeStruct((block, HD), jnp.bfloat16)] * 4,
        scratch_shapes=[
            pltpu.VMEM((4, block, HD), jnp.bfloat16),
            pltpu.VMEM((count, block, 2 * HD), jnp.bfloat16),
        ],
        compiler_params=pltpu.CompilerParams(vmem_limit_bytes=VMEM),
        cost_estimate=pl.CostEstimate(flops=12000000000 if high else 6000000000, bytes_accessed=1000, transcendentals=0),
        name="attend",
    )(meta, after, later, *pieces)


ORDER = (3, 1, 2, 0)


def finish_kernel(chunk, meta, ids, after, *refs):
    heads, (partner, own_w, other_w, to_x, to_y, keep_a, keep_b, rows) = refs[:4], refs[4:]
    step = pl.program_id(0)
    mine, seq = meta[0], meta[1]

    @pl.when(step == 0)
    def _():
        for j in range(4):
            same = ids[((chunk * 4 + seq) * 8 + 4 * mine + j) * SPAN] == mine
            at = pl.multiple_of((4 * mine + j) * SPAN, SPAN)
            for k in range(8):
                value = heads[k][pl.ds(at, SPAN), :] if k < 4 else partner[k - 4, j * SPAN : (j + 1) * SPAN, :]
                zero = jnp.zeros_like(value)
                head = (mine ^ (k // 4)) * 4 + (seq ^ (k % 4))
                lanes = pl.ds(pl.multiple_of(head * HD, HD), HD)
                rows[0, j * SPAN : (j + 1) * SPAN, lanes] = jnp.where(same, value, zero)
                rows[1, j * SPAN : (j + 1) * SPAN, lanes] = jnp.where(same, zero, value)

    term = jnp.dot(rows[0], own_w[...], preferred_element_type=jnp.float32)
    term += jnp.dot(rows[1], other_w[...], preferred_element_type=jnp.float32)
    term = term.astype(jnp.bfloat16)
    half = term.shape[0] // 2
    places = {
        0: ((keep_a, 0), (keep_b, 0)),
        1: ((to_x, 0), (keep_b, 1)),
        2: ((keep_a, 1), (to_y, 0)),
        3: ((to_x, 1), (to_y, 1)),
    }
    for at, k in enumerate(ORDER):

        @pl.when(step == at)
        def _():
            (a, i), (b, j) = places[k]
            a[i] = term[:half]
            b[j] = term[half:]


def finish(chunk, meta, ids, after, heads, own_w, other_w):
    depth, total = own_w.shape
    width = total // 4
    count = heads[-1].shape[1]
    whole = pl.BlockSpec(memory_space=pltpu.VMEM)

    def column(i, meta, ids):
        k = jnp.where(i == 0, 3, jnp.where(i == 3, 0, i))
        return (0, meta[2] ^ k)

    shape = jax.ShapeDtypeStruct((2, count // 2, width), jnp.bfloat16)
    return pl.pallas_call(
        partial(finish_kernel, chunk),
        grid_spec=pltpu.PrefetchScalarGridSpec(
            num_scalar_prefetch=2,
            grid=(4,),
            in_specs=[pl.BlockSpec(memory_space=pl.ANY)]
            + [whole] * 5
            + [pl.BlockSpec((depth, width), column), pl.BlockSpec((depth, width), column)],
            out_specs=[whole] * 4,
            scratch_shapes=[pltpu.VMEM((2, count, depth), jnp.bfloat16)],
        ),
        out_shape=[shape] * 4,
        compiler_params=pltpu.CompilerParams(vmem_limit_bytes=VMEM),
        cost_estimate=pl.CostEstimate(flops=12000000000, bytes_accessed=1000, transcendentals=0),
        name="finish",
    )(meta, ids, after, *heads, own_w, other_w)


def body(tokens, modality, norm_gain, input_weight, head_gain, output_weight):
    mine, seq, tp = lax.axis_index("mod"), lax.axis_index("seq"), lax.axis_index("tp")
    width = tokens.shape[1]
    half = input_weight.shape[3] // 2
    first = mine == 0
    meta = jnp.stack([mine, seq, tp]).astype(jnp.int32)

    def to_mod(value):
        return lax.ppermute(value, "mod", swap(2, 1))

    def to_x(value):
        return lax.ppermute(value, "tp", swap(4, 1))

    def to_y(value):
        return lax.ppermute(value, "tp", swap(4, 2))

    own_w = jnp.transpose(input_weight[0], (1, 0, 2))
    partner = to_mod(tokens)
    early_half = other_half(meta, [], own_w, (1,))
    partner, early_half = lax.optimization_barrier((partner, early_half))
    blocks = [jnp.where(first, tokens, partner), jnp.where(first, partner, tokens)]
    rows = blocks[0].shape[0] // 2
    quarter = rows // 2
    starts = [lax.dynamic_slice_in_dim(block, mine * rows, rows, axis=0) for block in blocks]
    low_x, low_y, early_w = to_x(starts[0]), to_y(starts[0]), to_mod(early_half)
    low_x, low_y, start_high = lax.optimization_barrier((low_x, low_y, starts[1]))
    late_w = [
        to_mod(other_half(meta, [starts[0]], own_w, (0,))),
        to_mod(other_half(meta, [low_x, low_y], own_w, (2,))),
    ]
    high_x, high_y = to_x(start_high), to_y(start_high)
    own_out = output_weight[0]
    arrived, projected = [], []
    for chunk, pieces in enumerate(([low_x, low_y], [high_x, high_y])):
        if chunk:
            pieces[0], pieces[1], late_out, _ = lax.optimization_barrier((high_x, high_y, own_out, projected[0]))
            other_out = to_mod(late_out)
        pieces = pieces + [to_y(pieces[0][:quarter]), to_x(pieces[1][quarter:])]
        q = to_mod(jnp.concatenate(pieces))
        pieces = [blocks[chunk]] + pieces + [q]
        sent = project(chunk, meta, modality, pieces, norm_gain, head_gain, own_w, early_w, late_w)
        projected.append(sent)
    arrived.append(lax.all_to_all(projected[0], "seq", 0, 0, tiled=True))
    low_mixed = attend(meta, projected[1], projected[1], arrived[0])

    def return_heads(mixed):
        return [mixed[0]] + [lax.ppermute(mixed[k], "seq", swap(4, k)) for k in (1, 2, 3)]

    low_heads = return_heads(low_mixed)
    projected[1], *low_heads = lax.optimization_barrier((projected[1], *low_heads))
    arrived.append(lax.all_to_all(projected[1], "seq", 0, 0, tiled=True))

    def output_rows(chunk, heads, after):
        cut = [lax.dynamic_slice_in_dim(head, (1 - mine) * rows, rows, axis=0) for head in heads]
        heads = heads + [to_mod(jnp.stack(cut))]
        send_x, send_y, keep_a, keep_b = finish(chunk, meta, modality, after, heads, own_out, other_out)
        got_x, got_y = to_x(send_x), to_y(send_y)
        return got_x, got_y, keep_a, keep_b

    def added(got_x, got_y, keep_a, keep_b):
        got_x, got_y, keep_a, keep_b = [part.astype(jnp.float32) for part in (got_x, got_y, keep_a, keep_b)]
        last_a = to_y((keep_a[1] + got_x[1]).astype(jnp.bfloat16)).astype(jnp.float32)
        last_b = to_x((keep_b[1] + got_y[1]).astype(jnp.bfloat16)).astype(jnp.float32)
        result = jnp.concatenate([keep_a[0] + got_x[0] + last_a, keep_b[0] + got_y[0] + last_b])
        return result.astype(jnp.bfloat16)

    low_rows = output_rows(0, low_heads, other_out)
    high_mixed = attend(meta, low_rows[0], low_rows[1], *arrived)
    high_rows = output_rows(1, return_heads(high_mixed), high_mixed[0])
    results = [added(*low_rows), added(*high_rows)]
    back = to_mod(jnp.where(first, results[1], results[0]))
    return jnp.concatenate(
        [jnp.where(first, results[0], back), jnp.where(first, back, results[1])], axis=0
    )


def solution(mesh):
    sizes = dict(mesh.shape)
    in_specs = (
        P(("mod", "seq"), "tp"),
        P(),
        P(),
        P("mod", None, None, "tp"),
        P(),
        P("mod", "tp", None),
    )
    out_specs = P(("mod", "seq"), "tp")

    def run(tokens, modality, norm_gain, input_weight, head_gain, output_weight):
        heads = input_weight.shape[3] // HD
        shard = tokens.shape[0] // (sizes["mod"] * sizes["seq"])
        small = (sizes["mod"], sizes["seq"], sizes["tp"]) == (2, 4, 4)
        fits = small and heads == 32 and shard == 8 * SPAN
        return jax.shard_map(
            body if fits else general_body,
            mesh=mesh,
            in_specs=in_specs,
            out_specs=out_specs,
            check_vma=False,
        )(tokens, modality, norm_gain, input_weight, head_gain, output_weight)

    return run
```

```python
from functools import partial
import math

import jax
import jax.numpy as jnp
from jax import lax
from jax.experimental import pallas as pl
from jax.experimental.pallas import tpu as pltpu
from jax.sharding import PartitionSpec as P

HD = 128
CAP = 320
SPAN = 64
SLOTS = CAP // SPAN
VMEM = 40 * 1024 * 1024


epsilon = 1e-05
sentinel = 1 << 30


def route_table(shard_ids, shard_index, slot_count):
    length = shard_ids.shape[0]
    order = jnp.argsort(shard_ids, stable=True)
    text_count = jnp.sum((shard_ids == 0).astype(jnp.int32))
    padded = jnp.concatenate([order, jnp.zeros((slot_count,), jnp.int32)])
    slot_index = jnp.arange(slot_count, dtype=jnp.int32)
    picked = jnp.stack(
        [padded[:slot_count], lax.dynamic_slice_in_dim(padded, text_count, slot_count)]
    )
    live = jnp.stack([slot_index < text_count, slot_index < length - text_count])
    place = shard_index * length + picked
    query_place = jnp.where(live, place, -1)
    key_place = jnp.where(live, place, sentinel)
    return (order, text_count, picked, live, query_place, key_place)


def select_rows(table, picked, live):
    return jnp.where(live[:, :, None], table[picked], jnp.zeros((), table.dtype))


def head_norm(part, gain):
    return part * lax.rsqrt(jnp.mean(part * part, axis=-1, keepdims=True) + epsilon) * gain


def general_body(tokens, modality, norm_gain, input_weight, head_gain, output_weight):
    length = tokens.shape[0]
    mod_count = lax.axis_size("mod")
    seq_count = lax.axis_size("seq")
    shards = mod_count * seq_count
    mine = lax.axis_index("mod")
    seq_index = lax.axis_index("seq")
    all_ids = modality.reshape(shards, length)
    own_index = mine * seq_count + seq_index
    own_ids = lax.dynamic_index_in_dim(all_ids, own_index, 0, keepdims=False)
    own_table = route_table(own_ids, own_index, CAP)
    order = own_table[0]
    text_count = own_table[1]
    picked = own_table[2]
    live = own_table[3]
    tables = jax.vmap(partial(route_table, slot_count=CAP))(
        all_ids, jnp.arange(shards, dtype=jnp.int32)
    )
    query_grid = tables[4].reshape(mod_count, seq_count, 2, CAP)
    own_query = lax.dynamic_index_in_dim(query_grid, seq_index, 1, keepdims=False)
    own_query = lax.dynamic_index_in_dim(own_query, mine, 1, keepdims=False).reshape(
        mod_count * CAP
    )
    key_grid = tables[5].reshape(mod_count, seq_count, 2, CAP)
    key_order = jnp.transpose(key_grid, (2, 1, 0, 3)).reshape(shards * mod_count * CAP)
    gathered = lax.all_gather(tokens, "tp", axis=1, tiled=True)
    arrived = lax.all_to_all(
        select_rows(gathered, picked, live), "mod", split_axis=0, concat_axis=0, tiled=True
    )
    rows_total = arrived.shape[0] * arrived.shape[1]
    width = arrived.shape[2]
    states = arrived.reshape(rows_total, width).astype(jnp.float32)
    gain = lax.dynamic_index_in_dim(norm_gain, mine, 0, keepdims=False)
    normed = (
        states * lax.rsqrt(jnp.mean(states * states, axis=1, keepdims=True) + epsilon) * gain
    ).astype(jnp.bfloat16)
    local_width = input_weight.shape[3]
    heads_here = local_width // HD
    projected = jnp.dot(
        normed, input_weight[0].reshape(width, 3 * local_width), preferred_element_type=jnp.float32
    )
    projected = projected.reshape(rows_total, 3, heads_here, HD)
    gains = lax.dynamic_index_in_dim(head_gain, mine, 0, keepdims=False)
    query_rows = head_norm(projected[:, 0], gains[0]).astype(jnp.bfloat16)
    key_rows = (
        head_norm(projected[:, 1], gains[1]).astype(jnp.bfloat16).reshape(rows_total, local_width)
    )
    value_rows = projected[:, 2].astype(jnp.bfloat16).reshape(rows_total, local_width)
    scale = 1.0 / math.sqrt(HD)
    key_piece = lax.all_gather(key_rows, ("mod", "seq"), axis=0, tiled=True)
    value_piece = lax.all_gather(value_rows, ("mod", "seq"), axis=0, tiled=True)
    count = key_piece.shape[0]
    scores = (
        jnp.einsum(
            "rhe,khe->hrk",
            query_rows,
            key_piece.reshape(count, heads_here, HD),
            preferred_element_type=jnp.float32,
        )
        * scale
    )
    weights = jnp.where(key_order[None, None, :] <= own_query[None, :, None], jnp.exp(scores), 0.0)
    totals = jnp.sum(weights, axis=2)
    rounded = weights.astype(jnp.bfloat16)
    weighted = jnp.einsum(
        "hrk,khe->rhe",
        rounded,
        value_piece.reshape(count, heads_here, HD),
        preferred_element_type=jnp.float32,
    )
    weighted, totals = (weighted, totals)
    totals = jnp.where(own_query[None, :] >= 0, totals, 1.0)
    attention = (
        (weighted / jnp.transpose(totals)[:, :, None])
        .astype(jnp.bfloat16)
        .reshape(rows_total, local_width)
    )
    head_terms = jnp.dot(attention, output_weight[0], preferred_element_type=jnp.float32)
    summed = lax.psum_scatter(
        head_terms.astype(jnp.bfloat16), "tp", scatter_dimension=1, tiled=True
    ).astype(jnp.float32)
    result = summed.astype(jnp.bfloat16).reshape(mod_count, CAP, summed.shape[1])
    returned = lax.all_to_all(result, "mod", split_axis=0, concat_axis=0, tiled=True)
    flat = returned.reshape(mod_count * CAP, summed.shape[1])
    inverse = jnp.zeros((length,), jnp.int32).at[order].set(jnp.arange(length, dtype=jnp.int32))
    slot = own_ids * CAP + inverse - own_ids * text_count
    return flat[slot]


def swap(size, bit):
    return [(i, i ^ bit) for i in range(size)]


def half_kernel(parts, meta, weight, *refs):
    out, held, come, gone = refs[-4:]
    half = out.shape[2]
    depth = held.shape[1]
    start = pl.multiple_of((1 - meta[0]) * half, half)
    inward, outward = [], []
    for n, part in enumerate(parts):
        for f in range(out.shape[1] // depth):
            at, deep = len(inward), pl.ds(f * depth, depth)
            source = weight.at[part, deep, pl.ds(start, half)]
            inward.append(pltpu.make_async_copy(source, held.at[at], come.at[at]))
            outward.append(pltpu.make_async_copy(held.at[at], out.at[n, deep, :], gone.at[at]))
    for copy in inward:
        copy.start()
    for first, second in zip(inward, outward):
        first.wait()
        second.start()
    for copy in outward:
        copy.wait()


def other_half(meta, after, weight, parts):
    outside = pl.BlockSpec(memory_space=pl.ANY)
    depth, half = weight.shape[1], weight.shape[2] // 2
    count = 4 * len(parts)
    return pl.pallas_call(
        partial(half_kernel, parts),
        in_specs=[pl.BlockSpec(memory_space=pltpu.SMEM)] + [outside] * (1 + len(after)),
        out_specs=outside,
        out_shape=jax.ShapeDtypeStruct((len(parts), depth, half), weight.dtype),
        scratch_shapes=[
            pltpu.VMEM((count, depth // 4, half), weight.dtype),
            pltpu.SemaphoreType.DMA((count,)),
            pltpu.SemaphoreType.DMA((count,)),
        ],
        compiler_params=pltpu.CompilerParams(vmem_limit_bytes=VMEM),
        cost_estimate=pl.CostEstimate(flops=count * 1000000000, bytes_accessed=1000, transcendentals=0),
        name="other_half",
    )(meta, weight, *after)


def project_kernel(chunk, meta, ids, block, p1, p2, p3a, p3b, q, gain, head_gain, own_w, early_w, query_w, value_w, out, rows, inverse, tiles, held, table, sems):
    mine, seq, tp = meta[0], meta[1], meta[2]
    width, half = tiles.shape[2:]
    features = 4 * width
    count = block.shape[0]
    incoming, place = [], 0
    for n, piece in enumerate((block, p1, p2, p3a, p3b, q)):
        incoming.append(
            pltpu.make_async_copy(piece, held.at[pl.ds(place, piece.shape[0]), :], sems.at[8 + n])
        )
        place += piece.shape[0]
    for copy in incoming:
        copy.start()

    def part_of(step):
        which = lax.rem(step, 3)
        return jnp.where(which == 0, 1, jnp.where(which == 1, 0, 2))

    def copies(step, act):
        which = lax.rem(step, 3)
        for f in range(4):
            deep = pl.ds(f * width, width)
            slot = lax.rem(step, 2) * 4 + f

            def move(source):
                act(pltpu.make_async_copy(source, tiles.at[lax.rem(step, 2), f], sems.at[slot]))

            @pl.when(step < 3)
            def _():
                move(own_w.at[part_of(step), deep, pl.ds(pl.multiple_of(mine * half, half), half)])

            @pl.when(step == 3)
            def _():
                move(early_w.at[0, deep, :])

            @pl.when(step == 4)
            def _():
                move(query_w.at[0, deep, :])

            @pl.when(step == 5)
            def _():
                move(value_w.at[0, deep, :])

    for step in range(2):
        copies(jnp.int32(step), lambda copy: copy.start())
    for copy in incoming:
        copy.wait()
    counts = [jnp.int32(0), jnp.int32(0)]
    for j in range(8):
        near, at = j < 4, j % 4
        span = 4 * mine + at if near else 4 * (1 - mine) + at
        kind = ids[((chunk * 4 + seq) * 8 + span) * SPAN]
        same = (kind == mine).astype(jnp.int32)
        group = 1 - same
        slot = jnp.where(same == 1, counts[0], counts[1])
        counts = [counts[0] + same, counts[1] + group]
        table[group * 8 + slot] = span
        place = pl.ds(pl.multiple_of(slot * SPAN, SPAN), SPAN)
        total = jnp.zeros((SPAN, 1), jnp.float32)
        for k in range(4):
            if k == 0:
                value = held[pl.ds(pl.multiple_of(span * SPAN, SPAN), SPAN), :]
            else:
                start = count + (0 if near else 3 * count // 2) + (k - 1) * count // 2 + at * SPAN
                value = held[start : start + SPAN, :]
            value = value.astype(jnp.float32)
            total += jnp.sum(value * value, axis=1, keepdims=True)
            feature = tp ^ k
            scale = gain[pl.ds(kind, 1), pl.ds(pl.multiple_of(feature * width, width), width)]
            rows[feature, group, place, :] = (value * scale).astype(jnp.bfloat16)
        scale = lax.rsqrt(total / features + epsilon)
        inverse[group, place, :] = jnp.broadcast_to(scale, (SPAN, HD))
    table[16] = counts[0]
    table[17] = counts[1]

    @pl.loop(0, 6, unroll=True)
    def _(step):
        group = (step >= 3).astype(jnp.int32)
        copies(step, lambda copy: copy.wait())
        buffer = lax.rem(step, 2)
        total = None
        for f in range(4):
            term = jnp.dot(rows[f, group], tiles[buffer, f], preferred_element_type=jnp.float32)
            total = term if total is None else total + term
        @pl.when(step < 4)
        def _():
            copies(step + 2, lambda copy: copy.start())

        kind = jnp.where(group == 0, mine, 1 - mine)
        which = part_of(step)
        scale = inverse[group]
        count = table[16 + group]
        row = head_gain[kind, pl.ds(jnp.minimum(which, 1), 1), :]
        row = row * jnp.where(which == 0, math.log2(math.e) / math.sqrt(HD), 1.0)
        for h in range(4):
            piece = total[:, h * HD : (h + 1) * HD] * scale
            mean = jnp.mean(piece * piece, axis=1, keepdims=True)
            normed = piece * lax.rsqrt(mean + epsilon) * row
            value = jnp.where(which == 2, piece, normed).astype(jnp.bfloat16)
            for slot in range(SLOTS):

                @pl.when(slot < count)
                def _():
                    span = table[group * 8 + slot]
                    out[h, which, pl.ds(pl.multiple_of(span * SPAN, SPAN), SPAN), :] = value[
                        slot * SPAN : (slot + 1) * SPAN
                    ]


def project(chunk, meta, ids, pieces, gain, head_gain, own_w, early_w, late_w):
    depth, half = early_w.shape[1:]
    width = depth // 4
    whole = pl.BlockSpec(memory_space=pltpu.VMEM)
    scalars = pl.BlockSpec(memory_space=pltpu.SMEM)
    outside = pl.BlockSpec(memory_space=pl.ANY)
    shape = jax.ShapeDtypeStruct((4, 3, 8 * SPAN, HD), jnp.bfloat16)
    return pl.pallas_call(
        partial(project_kernel, chunk),
        in_specs=[scalars] * 2 + [outside] * 6 + [whole] * 2 + [outside] * 4,
        out_specs=whole,
        scratch_shapes=[
            pltpu.VMEM((4, 2, CAP, width), jnp.bfloat16),
            pltpu.VMEM((2, CAP, HD), jnp.float32),
            pltpu.VMEM((2, 4, width, half), jnp.bfloat16),
            pltpu.VMEM((4 * 8 * SPAN, width), jnp.bfloat16),
            pltpu.SMEM((32,), jnp.int32),
            pltpu.SemaphoreType.DMA((14,)),
        ],
        out_shape=shape,
        compiler_params=pltpu.CompilerParams(vmem_limit_bytes=VMEM),
        cost_estimate=pl.CostEstimate(flops=1000, bytes_accessed=1000, transcendentals=0),
        name="project",
    )(meta, ids, *pieces, gain, head_gain, own_w, early_w, *late_w)


def attend_kernel(high, meta, after, later, *refs):
    first, last = refs[0], refs[1] if high else refs[0]
    outs, (mixed, values) = refs[-6:-2], refs[-2:]
    seq = meta[1]
    block = last.shape[2]
    half = block // 2
    for base, pieces in ((0, first), (4, last)) if high else ((0, first),):
        for at in range(4):
            values[base + at, :, :HD] = pieces[at, 2]
            values[base + at, :, HD:] = jnp.ones((block, HD), jnp.bfloat16)
    diagonal = lax.broadcasted_iota(jnp.int32, (half, half), 0) >= lax.broadcasted_iota(
        jnp.int32, (half, half), 1
    )

    def scores(query, key):
        return lax.dot_general(query, key, (((1,), (1,)), ((), ())), preferred_element_type=jnp.float32)

    for at in range(4):
        own = 4 + at if high else at
        for side in range(2):
            query = last[at, 0, side * half : (side + 1) * half, :]
            weight = jnp.where(
                diagonal, jnp.exp2(scores(query, last[at, 1, side * half : (side + 1) * half, :])), 0.0
            ).astype(jnp.bfloat16)
            total = jnp.dot(
                weight, values[own, side * half : (side + 1) * half, :], preferred_element_type=jnp.float32
            )
            if side == 1:
                weight = jnp.exp2(scores(query, last[at, 1, :half, :])).astype(jnp.bfloat16)
                total += jnp.dot(weight, values[own, :half, :], preferred_element_type=jnp.float32)

            for j in range(own):
                key = first[j, 1] if j < 4 else last[j - 4, 1]
                weight = jnp.exp2(scores(query, key)).astype(jnp.bfloat16)
                total += jnp.dot(weight, values[j], preferred_element_type=jnp.float32)
            mixed[at, side * half : (side + 1) * half, :] = (total[:, :HD] / total[:, HD:]).astype(jnp.bfloat16)
    for k, out in enumerate(outs):
        out[...] = mixed[seq ^ k]


def attend(meta, after, later, first, last=None):
    high = last is not None
    pieces = [first, last] if high else [first]
    block = first.shape[2]
    whole = pl.BlockSpec(memory_space=pltpu.VMEM)
    count = 8 if high else 4
    return pl.pallas_call(
        partial(attend_kernel, high),
        in_specs=[pl.BlockSpec(memory_space=pltpu.SMEM)]
        + [pl.BlockSpec(memory_space=pl.ANY)] * 2
        + [whole] * len(pieces),
        out_specs=[whole] * 4,
        out_shape=[jax.ShapeDtypeStruct((block, HD), jnp.bfloat16)] * 4,
        scratch_shapes=[
            pltpu.VMEM((4, block, HD), jnp.bfloat16),
            pltpu.VMEM((count, block, 2 * HD), jnp.bfloat16),
        ],
        compiler_params=pltpu.CompilerParams(vmem_limit_bytes=VMEM),
        cost_estimate=pl.CostEstimate(flops=12000000000 if high else 6000000000, bytes_accessed=1000, transcendentals=0),
        name="attend",
    )(meta, after, later, *pieces)


ORDER = (3, 1, 2, 0)


def finish_kernel(chunk, meta, ids, after, *refs):
    heads, (partner, own_w, other_w, to_x, to_y, keep_a, keep_b, rows) = refs[:4], refs[4:]
    step = pl.program_id(0)
    mine, seq = meta[0], meta[1]

    @pl.when(step == 0)
    def _():
        for j in range(4):
            same = ids[((chunk * 4 + seq) * 8 + 4 * mine + j) * SPAN] == mine
            at = pl.multiple_of((4 * mine + j) * SPAN, SPAN)
            for k in range(8):
                value = heads[k][pl.ds(at, SPAN), :] if k < 4 else partner[k - 4, j * SPAN : (j + 1) * SPAN, :]
                zero = jnp.zeros_like(value)
                head = (mine ^ (k // 4)) * 4 + (seq ^ (k % 4))
                lanes = pl.ds(pl.multiple_of(head * HD, HD), HD)
                rows[0, j * SPAN : (j + 1) * SPAN, lanes] = jnp.where(same, value, zero)
                rows[1, j * SPAN : (j + 1) * SPAN, lanes] = jnp.where(same, zero, value)

    term = jnp.dot(rows[0], own_w[...], preferred_element_type=jnp.float32)
    term += jnp.dot(rows[1], other_w[...], preferred_element_type=jnp.float32)
    term = term.astype(jnp.bfloat16)
    half = term.shape[0] // 2
    places = {
        0: ((keep_a, 0), (keep_b, 0)),
        1: ((to_x, 0), (keep_b, 1)),
        2: ((keep_a, 1), (to_y, 0)),
        3: ((to_x, 1), (to_y, 1)),
    }
    for at, k in enumerate(ORDER):

        @pl.when(step == at)
        def _():
            (a, i), (b, j) = places[k]
            a[i] = term[:half]
            b[j] = term[half:]


def finish(chunk, meta, ids, after, heads, own_w, other_w):
    depth, total = own_w.shape
    width = total // 4
    count = heads[-1].shape[1]
    whole = pl.BlockSpec(memory_space=pltpu.VMEM)

    def column(i, meta, ids):
        k = jnp.where(i == 0, 3, jnp.where(i == 3, 0, i))
        return (0, meta[2] ^ k)

    shape = jax.ShapeDtypeStruct((2, count // 2, width), jnp.bfloat16)
    return pl.pallas_call(
        partial(finish_kernel, chunk),
        grid_spec=pltpu.PrefetchScalarGridSpec(
            num_scalar_prefetch=2,
            grid=(4,),
            in_specs=[pl.BlockSpec(memory_space=pl.ANY)]
            + [whole] * 5
            + [pl.BlockSpec((depth, width), column), pl.BlockSpec((depth, width), column)],
            out_specs=[whole] * 4,
            scratch_shapes=[pltpu.VMEM((2, count, depth), jnp.bfloat16)],
        ),
        out_shape=[shape] * 4,
        compiler_params=pltpu.CompilerParams(vmem_limit_bytes=VMEM),
        cost_estimate=pl.CostEstimate(flops=12000000000, bytes_accessed=1000, transcendentals=0),
        name="finish",
    )(meta, ids, after, *heads, own_w, other_w)


def body(tokens, modality, norm_gain, input_weight, head_gain, output_weight):
    mine, seq, tp = lax.axis_index("mod"), lax.axis_index("seq"), lax.axis_index("tp")
    width = tokens.shape[1]
    half = input_weight.shape[3] // 2
    first = mine == 0
    meta = jnp.stack([mine, seq, tp]).astype(jnp.int32)

    def to_mod(value):
        return lax.ppermute(value, "mod", swap(2, 1))

    def to_x(value):
        return lax.ppermute(value, "tp", swap(4, 1))

    def to_y(value):
        return lax.ppermute(value, "tp", swap(4, 2))

    own_w = jnp.transpose(input_weight[0], (1, 0, 2))
    partner = to_mod(tokens)
    early_half = other_half(meta, [], own_w, (1,))
    partner, early_half = lax.optimization_barrier((partner, early_half))
    blocks = [jnp.where(first, tokens, partner), jnp.where(first, partner, tokens)]
    rows = blocks[0].shape[0] // 2
    quarter = rows // 2
    starts = [lax.dynamic_slice_in_dim(block, mine * rows, rows, axis=0) for block in blocks]
    low_x, low_y, early_w = to_x(starts[0]), to_y(starts[0]), to_mod(early_half)
    low_x, low_y, start_high = lax.optimization_barrier((low_x, low_y, starts[1]))
    late_w = [
        to_mod(other_half(meta, [starts[0]], own_w, (0,))),
        to_mod(other_half(meta, [low_x, low_y], own_w, (2,))),
    ]
    high_x, high_y = to_x(start_high), to_y(start_high)
    own_out = output_weight[0]
    arrived, projected = [], []
    for chunk, pieces in enumerate(([low_x, low_y], [high_x, high_y])):
        if chunk:
            pieces[0], pieces[1], late_out, _ = lax.optimization_barrier((high_x, high_y, own_out, projected[0]))
            other_out = to_mod(late_out)
        pieces = pieces + [to_y(pieces[0][:quarter]), to_x(pieces[1][quarter:])]
        q = to_mod(jnp.concatenate(pieces))
        pieces = [blocks[chunk]] + pieces + [q]
        sent = project(chunk, meta, modality, pieces, norm_gain, head_gain, own_w, early_w, late_w)
        projected.append(sent)
    arrived.append(lax.all_to_all(projected[0], "seq", 0, 0, tiled=True))
    low_mixed = attend(meta, projected[1], projected[1], arrived[0])

    def return_heads(mixed):
        return [mixed[0]] + [lax.ppermute(mixed[k], "seq", swap(4, k)) for k in (1, 2, 3)]

    arrived.append(lax.all_to_all(projected[1], "seq", 0, 0, tiled=True))
    arrived[1], *low_mixed = lax.optimization_barrier((arrived[1], *low_mixed))
    low_heads = return_heads(low_mixed)
    high_mixed = attend(meta, other_out, other_out, *arrived)
    high_heads = return_heads(high_mixed)
    *low_heads, _ = lax.optimization_barrier((*low_heads, high_mixed[0]))

    def output_rows(chunk, heads, after):
        cut = [lax.dynamic_slice_in_dim(head, (1 - mine) * rows, rows, axis=0) for head in heads]
        heads = heads + [to_mod(jnp.stack(cut))]
        send_x, send_y, keep_a, keep_b = finish(chunk, meta, modality, after, heads, own_out, other_out)
        got_x, got_y = to_x(send_x), to_y(send_y)
        return got_x, got_y, keep_a, keep_b

    def added(got_x, got_y, keep_a, keep_b):
        got_x, got_y, keep_a, keep_b = [part.astype(jnp.float32) for part in (got_x, got_y, keep_a, keep_b)]
        last_a = to_y((keep_a[1] + got_x[1]).astype(jnp.bfloat16)).astype(jnp.float32)
        last_b = to_x((keep_b[1] + got_y[1]).astype(jnp.bfloat16)).astype(jnp.float32)
        result = jnp.concatenate([keep_a[0] + got_x[0] + last_a, keep_b[0] + got_y[0] + last_b])
        return result.astype(jnp.bfloat16)

    low_rows = output_rows(0, low_heads, high_heads[1])
    high_rows = output_rows(1, high_heads, low_rows[2])
    results = [added(*low_rows), added(*high_rows)]
    back = to_mod(jnp.where(first, results[1], results[0]))
    return jnp.concatenate(
        [jnp.where(first, results[0], back), jnp.where(first, back, results[1])], axis=0
    )


def solution(mesh):
    sizes = dict(mesh.shape)
    in_specs = (
        P(("mod", "seq"), "tp"),
        P(),
        P(),
        P("mod", None, None, "tp"),
        P(),
        P("mod", "tp", None),
    )
    out_specs = P(("mod", "seq"), "tp")

    def run(tokens, modality, norm_gain, input_weight, head_gain, output_weight):
        heads = input_weight.shape[3] // HD
        shard = tokens.shape[0] // (sizes["mod"] * sizes["seq"])
        small = (sizes["mod"], sizes["seq"], sizes["tp"]) == (2, 4, 4)
        fits = small and heads == 32 and shard == 8 * SPAN
        return jax.shard_map(
            body if fits else general_body,
            mesh=mesh,
            in_specs=in_specs,
            out_specs=out_specs,
            check_vma=False,
        )(tokens, modality, norm_gain, input_weight, head_gain, output_weight)

    return run
```

```python
from functools import partial
import math

import jax
import jax.numpy as jnp
from jax import lax
from jax.experimental import pallas as pl
from jax.experimental.pallas import tpu as pltpu
from jax.sharding import PartitionSpec as P

HD = 128
CAP = 320
SPAN = 64
SLOTS = CAP // SPAN
VMEM = 40 * 1024 * 1024


epsilon = 1e-05
sentinel = 1 << 30


def route_table(shard_ids, shard_index, slot_count):
    length = shard_ids.shape[0]
    order = jnp.argsort(shard_ids, stable=True)
    text_count = jnp.sum((shard_ids == 0).astype(jnp.int32))
    padded = jnp.concatenate([order, jnp.zeros((slot_count,), jnp.int32)])
    slot_index = jnp.arange(slot_count, dtype=jnp.int32)
    picked = jnp.stack(
        [padded[:slot_count], lax.dynamic_slice_in_dim(padded, text_count, slot_count)]
    )
    live = jnp.stack([slot_index < text_count, slot_index < length - text_count])
    place = shard_index * length + picked
    query_place = jnp.where(live, place, -1)
    key_place = jnp.where(live, place, sentinel)
    return (order, text_count, picked, live, query_place, key_place)


def select_rows(table, picked, live):
    return jnp.where(live[:, :, None], table[picked], jnp.zeros((), table.dtype))


def head_norm(part, gain):
    return part * lax.rsqrt(jnp.mean(part * part, axis=-1, keepdims=True) + epsilon) * gain


def general_body(tokens, modality, norm_gain, input_weight, head_gain, output_weight):
    length = tokens.shape[0]
    mod_count = lax.axis_size("mod")
    seq_count = lax.axis_size("seq")
    shards = mod_count * seq_count
    mine = lax.axis_index("mod")
    seq_index = lax.axis_index("seq")
    all_ids = modality.reshape(shards, length)
    own_index = mine * seq_count + seq_index
    own_ids = lax.dynamic_index_in_dim(all_ids, own_index, 0, keepdims=False)
    own_table = route_table(own_ids, own_index, CAP)
    order = own_table[0]
    text_count = own_table[1]
    picked = own_table[2]
    live = own_table[3]
    tables = jax.vmap(partial(route_table, slot_count=CAP))(
        all_ids, jnp.arange(shards, dtype=jnp.int32)
    )
    query_grid = tables[4].reshape(mod_count, seq_count, 2, CAP)
    own_query = lax.dynamic_index_in_dim(query_grid, seq_index, 1, keepdims=False)
    own_query = lax.dynamic_index_in_dim(own_query, mine, 1, keepdims=False).reshape(
        mod_count * CAP
    )
    key_grid = tables[5].reshape(mod_count, seq_count, 2, CAP)
    key_order = jnp.transpose(key_grid, (2, 1, 0, 3)).reshape(shards * mod_count * CAP)
    gathered = lax.all_gather(tokens, "tp", axis=1, tiled=True)
    arrived = lax.all_to_all(
        select_rows(gathered, picked, live), "mod", split_axis=0, concat_axis=0, tiled=True
    )
    rows_total = arrived.shape[0] * arrived.shape[1]
    width = arrived.shape[2]
    states = arrived.reshape(rows_total, width).astype(jnp.float32)
    gain = lax.dynamic_index_in_dim(norm_gain, mine, 0, keepdims=False)
    normed = (
        states * lax.rsqrt(jnp.mean(states * states, axis=1, keepdims=True) + epsilon) * gain
    ).astype(jnp.bfloat16)
    local_width = input_weight.shape[3]
    heads_here = local_width // HD
    projected = jnp.dot(
        normed, input_weight[0].reshape(width, 3 * local_width), preferred_element_type=jnp.float32
    )
    projected = projected.reshape(rows_total, 3, heads_here, HD)
    gains = lax.dynamic_index_in_dim(head_gain, mine, 0, keepdims=False)
    query_rows = head_norm(projected[:, 0], gains[0]).astype(jnp.bfloat16)
    key_rows = (
        head_norm(projected[:, 1], gains[1]).astype(jnp.bfloat16).reshape(rows_total, local_width)
    )
    value_rows = projected[:, 2].astype(jnp.bfloat16).reshape(rows_total, local_width)
    scale = 1.0 / math.sqrt(HD)
    key_piece = lax.all_gather(key_rows, ("mod", "seq"), axis=0, tiled=True)
    value_piece = lax.all_gather(value_rows, ("mod", "seq"), axis=0, tiled=True)
    count = key_piece.shape[0]
    scores = (
        jnp.einsum(
            "rhe,khe->hrk",
            query_rows,
            key_piece.reshape(count, heads_here, HD),
            preferred_element_type=jnp.float32,
        )
        * scale
    )
    weights = jnp.where(key_order[None, None, :] <= own_query[None, :, None], jnp.exp(scores), 0.0)
    totals = jnp.sum(weights, axis=2)
    rounded = weights.astype(jnp.bfloat16)
    weighted = jnp.einsum(
        "hrk,khe->rhe",
        rounded,
        value_piece.reshape(count, heads_here, HD),
        preferred_element_type=jnp.float32,
    )
    weighted, totals = (weighted, totals)
    totals = jnp.where(own_query[None, :] >= 0, totals, 1.0)
    attention = (
        (weighted / jnp.transpose(totals)[:, :, None])
        .astype(jnp.bfloat16)
        .reshape(rows_total, local_width)
    )
    head_terms = jnp.dot(attention, output_weight[0], preferred_element_type=jnp.float32)
    summed = lax.psum_scatter(
        head_terms.astype(jnp.bfloat16), "tp", scatter_dimension=1, tiled=True
    ).astype(jnp.float32)
    result = summed.astype(jnp.bfloat16).reshape(mod_count, CAP, summed.shape[1])
    returned = lax.all_to_all(result, "mod", split_axis=0, concat_axis=0, tiled=True)
    flat = returned.reshape(mod_count * CAP, summed.shape[1])
    inverse = jnp.zeros((length,), jnp.int32).at[order].set(jnp.arange(length, dtype=jnp.int32))
    slot = own_ids * CAP + inverse - own_ids * text_count
    return flat[slot]


def swap(size, bit):
    return [(i, i ^ bit) for i in range(size)]


def half_kernel(parts, meta, weight, *refs):
    out, held, come, gone = refs[-4:]
    half = out.shape[2]
    depth = held.shape[1]
    start = pl.multiple_of((1 - meta[0]) * half, half)
    inward, outward = [], []
    for n, part in enumerate(parts):
        for f in range(out.shape[1] // depth):
            at, deep = len(inward), pl.ds(f * depth, depth)
            source = weight.at[part, deep, pl.ds(start, half)]
            inward.append(pltpu.make_async_copy(source, held.at[at], come.at[at]))
            outward.append(pltpu.make_async_copy(held.at[at], out.at[n, deep, :], gone.at[at]))
    for copy in inward:
        copy.start()
    for first, second in zip(inward, outward):
        first.wait()
        second.start()
    for copy in outward:
        copy.wait()


def other_half(meta, after, weight, parts):
    outside = pl.BlockSpec(memory_space=pl.ANY)
    depth, half = weight.shape[1], weight.shape[2] // 2
    count = 4 * len(parts)
    return pl.pallas_call(
        partial(half_kernel, parts),
        in_specs=[pl.BlockSpec(memory_space=pltpu.SMEM)] + [outside] * (1 + len(after)),
        out_specs=outside,
        out_shape=jax.ShapeDtypeStruct((len(parts), depth, half), weight.dtype),
        scratch_shapes=[
            pltpu.VMEM((count, depth // 4, half), weight.dtype),
            pltpu.SemaphoreType.DMA((count,)),
            pltpu.SemaphoreType.DMA((count,)),
        ],
        compiler_params=pltpu.CompilerParams(vmem_limit_bytes=VMEM),
        cost_estimate=pl.CostEstimate(flops=count * 1000000000, bytes_accessed=1000, transcendentals=0),
        name="other_half",
    )(meta, weight, *after)


def project_kernel(chunk, meta, ids, block, p1, p2, p3a, p3b, q, gain, head_gain, own_w, early_w, query_w, value_w, out, rows, inverse, tiles, held, table, sems):
    mine, seq, tp = meta[0], meta[1], meta[2]
    width, half = tiles.shape[2:]
    features = 4 * width
    count = block.shape[0]
    incoming, place = [], 0
    for n, piece in enumerate((block, p1, p2, p3a, p3b, q)):
        incoming.append(
            pltpu.make_async_copy(piece, held.at[pl.ds(place, piece.shape[0]), :], sems.at[8 + n])
        )
        place += piece.shape[0]
    for copy in incoming:
        copy.start()

    def part_of(step):
        which = lax.rem(step, 3)
        return jnp.where(which == 0, 1, jnp.where(which == 1, 0, 2))

    def copies(step, act):
        which = lax.rem(step, 3)
        for f in range(4):
            deep = pl.ds(f * width, width)
            slot = lax.rem(step, 2) * 4 + f

            def move(source):
                act(pltpu.make_async_copy(source, tiles.at[lax.rem(step, 2), f], sems.at[slot]))

            @pl.when(step < 3)
            def _():
                move(own_w.at[part_of(step), deep, pl.ds(pl.multiple_of(mine * half, half), half)])

            @pl.when(step == 3)
            def _():
                move(early_w.at[0, deep, :])

            @pl.when(step == 4)
            def _():
                move(query_w.at[0, deep, :])

            @pl.when(step == 5)
            def _():
                move(value_w.at[0, deep, :])

    for step in range(2):
        copies(jnp.int32(step), lambda copy: copy.start())
    for copy in incoming:
        copy.wait()
    counts = [jnp.int32(0), jnp.int32(0)]
    for j in range(8):
        near, at = j < 4, j % 4
        span = 4 * mine + at if near else 4 * (1 - mine) + at
        kind = ids[((chunk * 4 + seq) * 8 + span) * SPAN]
        same = (kind == mine).astype(jnp.int32)
        group = 1 - same
        slot = jnp.where(same == 1, counts[0], counts[1])
        counts = [counts[0] + same, counts[1] + group]
        table[group * 8 + slot] = span
        place = pl.ds(pl.multiple_of(slot * SPAN, SPAN), SPAN)
        total = jnp.zeros((SPAN, 1), jnp.float32)
        for k in range(4):
            if k == 0:
                value = held[pl.ds(pl.multiple_of(span * SPAN, SPAN), SPAN), :]
            else:
                start = count + (0 if near else 3 * count // 2) + (k - 1) * count // 2 + at * SPAN
                value = held[start : start + SPAN, :]
            value = value.astype(jnp.float32)
            total += jnp.sum(value * value, axis=1, keepdims=True)
            feature = tp ^ k
            scale = gain[pl.ds(kind, 1), pl.ds(pl.multiple_of(feature * width, width), width)]
            rows[feature, group, place, :] = (value * scale).astype(jnp.bfloat16)
        scale = lax.rsqrt(total / features + epsilon)
        inverse[group, place, :] = jnp.broadcast_to(scale, (SPAN, HD))
    table[16] = counts[0]
    table[17] = counts[1]

    @pl.loop(0, 6)
    def _(step):
        group = (step >= 3).astype(jnp.int32)
        copies(step, lambda copy: copy.wait())
        buffer = lax.rem(step, 2)
        total = None
        for f in range(4):
            term = jnp.dot(rows[f, group], tiles[buffer, f], preferred_element_type=jnp.float32)
            total = term if total is None else total + term
        @pl.when(step < 4)
        def _():
            copies(step + 2, lambda copy: copy.start())

        kind = jnp.where(group == 0, mine, 1 - mine)
        which = part_of(step)
        scale = inverse[group]
        count = table[16 + group]
        row = head_gain[kind, pl.ds(jnp.minimum(which, 1), 1), :]
        row = row * jnp.where(which == 0, math.log2(math.e) / math.sqrt(HD), 1.0)
        for h in range(4):
            piece = total[:, h * HD : (h + 1) * HD] * scale
            mean = jnp.mean(piece * piece, axis=1, keepdims=True)
            normed = piece * lax.rsqrt(mean + epsilon) * row
            value = jnp.where(which == 2, piece, normed).astype(jnp.bfloat16)
            for slot in range(SLOTS):

                @pl.when(slot < count)
                def _():
                    span = table[group * 8 + slot]
                    out[h, which, pl.ds(pl.multiple_of(span * SPAN, SPAN), SPAN), :] = value[
                        slot * SPAN : (slot + 1) * SPAN
                    ]


def project(chunk, meta, ids, pieces, gain, head_gain, own_w, early_w, late_w):
    depth, half = early_w.shape[1:]
    width = depth // 4
    whole = pl.BlockSpec(memory_space=pltpu.VMEM)
    scalars = pl.BlockSpec(memory_space=pltpu.SMEM)
    outside = pl.BlockSpec(memory_space=pl.ANY)
    shape = jax.ShapeDtypeStruct((4, 3, 8 * SPAN, HD), jnp.bfloat16)
    return pl.pallas_call(
        partial(project_kernel, chunk),
        in_specs=[scalars] * 2 + [outside] * 6 + [whole] * 2 + [outside] * 4,
        out_specs=whole,
        scratch_shapes=[
            pltpu.VMEM((4, 2, CAP, width), jnp.bfloat16),
            pltpu.VMEM((2, CAP, HD), jnp.float32),
            pltpu.VMEM((2, 4, width, half), jnp.bfloat16),
            pltpu.VMEM((4 * 8 * SPAN, width), jnp.bfloat16),
            pltpu.SMEM((32,), jnp.int32),
            pltpu.SemaphoreType.DMA((14,)),
        ],
        out_shape=shape,
        compiler_params=pltpu.CompilerParams(vmem_limit_bytes=VMEM),
        cost_estimate=pl.CostEstimate(flops=1000, bytes_accessed=1000, transcendentals=0),
        name="project",
    )(meta, ids, *pieces, gain, head_gain, own_w, early_w, *late_w)


def attend_kernel(high, meta, after, later, *refs):
    first, last = refs[0], refs[1] if high else refs[0]
    outs, (mixed, values) = refs[-6:-2], refs[-2:]
    seq = meta[1]
    block = last.shape[2]
    half = block // 2
    for base, pieces in ((0, first), (4, last)) if high else ((0, first),):
        for at in range(4):
            values[base + at, :, :HD] = pieces[at, 2]
            values[base + at, :, HD:] = jnp.ones((block, HD), jnp.bfloat16)
    diagonal = lax.broadcasted_iota(jnp.int32, (half, half), 0) >= lax.broadcasted_iota(
        jnp.int32, (half, half), 1
    )

    def scores(query, key):
        return lax.dot_general(query, key, (((1,), (1,)), ((), ())), preferred_element_type=jnp.float32)

    for at in range(4):
        own = 4 + at if high else at
        for side in range(2):
            query = last[at, 0, side * half : (side + 1) * half, :]
            weight = jnp.where(
                diagonal, jnp.exp2(scores(query, last[at, 1, side * half : (side + 1) * half, :])), 0.0
            ).astype(jnp.bfloat16)
            total = jnp.dot(
                weight, values[own, side * half : (side + 1) * half, :], preferred_element_type=jnp.float32
            )
            if side == 1:
                weight = jnp.exp2(scores(query, last[at, 1, :half, :])).astype(jnp.bfloat16)
                total += jnp.dot(weight, values[own, :half, :], preferred_element_type=jnp.float32)

            for j in range(own):
                key = first[j, 1] if j < 4 else last[j - 4, 1]
                weight = jnp.exp2(scores(query, key)).astype(jnp.bfloat16)
                total += jnp.dot(weight, values[j], preferred_element_type=jnp.float32)
            mixed[at, side * half : (side + 1) * half, :] = (total[:, :HD] / total[:, HD:]).astype(jnp.bfloat16)
    for k, out in enumerate(outs):
        out[...] = mixed[seq ^ k]


def attend(meta, after, later, first, last=None):
    high = last is not None
    pieces = [first, last] if high else [first]
    block = first.shape[2]
    whole = pl.BlockSpec(memory_space=pltpu.VMEM)
    count = 8 if high else 4
    return pl.pallas_call(
        partial(attend_kernel, high),
        in_specs=[pl.BlockSpec(memory_space=pltpu.SMEM)]
        + [pl.BlockSpec(memory_space=pl.ANY)] * 2
        + [whole] * len(pieces),
        out_specs=[whole] * 4,
        out_shape=[jax.ShapeDtypeStruct((block, HD), jnp.bfloat16)] * 4,
        scratch_shapes=[
            pltpu.VMEM((4, block, HD), jnp.bfloat16),
            pltpu.VMEM((count, block, 2 * HD), jnp.bfloat16),
        ],
        compiler_params=pltpu.CompilerParams(vmem_limit_bytes=VMEM),
        cost_estimate=pl.CostEstimate(flops=12000000000 if high else 6000000000, bytes_accessed=1000, transcendentals=0),
        name="attend",
    )(meta, after, later, *pieces)


ORDER = (3, 1, 2, 0)


def finish_kernel(chunk, meta, ids, after, *refs):
    heads, (partner, own_w, other_w, to_x, to_y, keep_a, keep_b, rows) = refs[:4], refs[4:]
    step = pl.program_id(0)
    mine, seq = meta[0], meta[1]

    @pl.when(step == 0)
    def _():
        for j in range(4):
            same = ids[((chunk * 4 + seq) * 8 + 4 * mine + j) * SPAN] == mine
            at = pl.multiple_of((4 * mine + j) * SPAN, SPAN)
            for k in range(8):
                value = heads[k][pl.ds(at, SPAN), :] if k < 4 else partner[k - 4, j * SPAN : (j + 1) * SPAN, :]
                zero = jnp.zeros_like(value)
                head = (mine ^ (k // 4)) * 4 + (seq ^ (k % 4))
                lanes = pl.ds(pl.multiple_of(head * HD, HD), HD)
                rows[0, j * SPAN : (j + 1) * SPAN, lanes] = jnp.where(same, value, zero)
                rows[1, j * SPAN : (j + 1) * SPAN, lanes] = jnp.where(same, zero, value)

    term = jnp.dot(rows[0], own_w[...], preferred_element_type=jnp.float32)
    term += jnp.dot(rows[1], other_w[...], preferred_element_type=jnp.float32)
    term = term.astype(jnp.bfloat16)
    half = term.shape[0] // 2
    places = {
        0: ((keep_a, 0), (keep_b, 0)),
        1: ((to_x, 0), (keep_b, 1)),
        2: ((keep_a, 1), (to_y, 0)),
        3: ((to_x, 1), (to_y, 1)),
    }
    for at, k in enumerate(ORDER):

        @pl.when(step == at)
        def _():
            (a, i), (b, j) = places[k]
            a[i] = term[:half]
            b[j] = term[half:]


def finish(chunk, meta, ids, after, heads, own_w, other_w):
    depth, total = own_w.shape
    width = total // 4
    count = heads[-1].shape[1]
    whole = pl.BlockSpec(memory_space=pltpu.VMEM)

    def column(i, meta, ids):
        k = jnp.where(i == 0, 3, jnp.where(i == 3, 0, i))
        return (0, meta[2] ^ k)

    shape = jax.ShapeDtypeStruct((2, count // 2, width), jnp.bfloat16)
    return pl.pallas_call(
        partial(finish_kernel, chunk),
        grid_spec=pltpu.PrefetchScalarGridSpec(
            num_scalar_prefetch=2,
            grid=(4,),
            in_specs=[pl.BlockSpec(memory_space=pl.ANY)]
            + [whole] * 5
            + [pl.BlockSpec((depth, width), column), pl.BlockSpec((depth, width), column)],
            out_specs=[whole] * 4,
            scratch_shapes=[pltpu.VMEM((2, count, depth), jnp.bfloat16)],
        ),
        out_shape=[shape] * 4,
        compiler_params=pltpu.CompilerParams(vmem_limit_bytes=VMEM),
        cost_estimate=pl.CostEstimate(flops=12000000000, bytes_accessed=1000, transcendentals=0),
        name="finish",
    )(meta, ids, after, *heads, own_w, other_w)


def body(tokens, modality, norm_gain, input_weight, head_gain, output_weight):
    mine, seq, tp = lax.axis_index("mod"), lax.axis_index("seq"), lax.axis_index("tp")
    width = tokens.shape[1]
    half = input_weight.shape[3] // 2
    first = mine == 0
    meta = jnp.stack([mine, seq, tp]).astype(jnp.int32)

    def to_mod(value):
        return lax.ppermute(value, "mod", swap(2, 1))

    def to_x(value):
        return lax.ppermute(value, "tp", swap(4, 1))

    def to_y(value):
        return lax.ppermute(value, "tp", swap(4, 2))

    own_w = jnp.transpose(input_weight[0], (1, 0, 2))
    partner = to_mod(tokens)
    early_half = other_half(meta, [], own_w, (1,))
    partner, early_half = lax.optimization_barrier((partner, early_half))
    blocks = [jnp.where(first, tokens, partner), jnp.where(first, partner, tokens)]
    rows = blocks[0].shape[0] // 2
    quarter = rows // 2
    starts = [lax.dynamic_slice_in_dim(block, mine * rows, rows, axis=0) for block in blocks]
    low_x, low_y, early_w = to_x(starts[0]), to_y(starts[0]), to_mod(early_half)
    low_x, low_y, start_high = lax.optimization_barrier((low_x, low_y, starts[1]))
    late_w = [
        to_mod(other_half(meta, [starts[0]], own_w, (0,))),
        to_mod(other_half(meta, [low_x, low_y], own_w, (2,))),
    ]
    high_x, high_y = to_x(start_high), to_y(start_high)
    own_out = output_weight[0]
    arrived, projected = [], []
    for chunk, pieces in enumerate(([low_x, low_y], [high_x, high_y])):
        if chunk:
            pieces[0], pieces[1], late_out, _ = lax.optimization_barrier((high_x, high_y, own_out, projected[0]))
            other_out = to_mod(late_out)
        pieces = pieces + [to_y(pieces[0][:quarter]), to_x(pieces[1][quarter:])]
        q = to_mod(jnp.concatenate(pieces))
        pieces = [blocks[chunk]] + pieces + [q]
        sent = project(chunk, meta, modality, pieces, norm_gain, head_gain, own_w, early_w, late_w)
        projected.append(sent)
    arrived.append(lax.all_to_all(projected[0], "seq", 0, 0, tiled=True))
    low_mixed = attend(meta, projected[1], projected[1], arrived[0])

    def return_heads(mixed):
        return [mixed[0]] + [lax.ppermute(mixed[k], "seq", swap(4, k)) for k in (1, 2, 3)]

    arrived.append(lax.all_to_all(projected[1], "seq", 0, 0, tiled=True))
    arrived[1], *low_mixed = lax.optimization_barrier((arrived[1], *low_mixed))
    low_heads = return_heads(low_mixed)
    high_mixed = attend(meta, other_out, other_out, *arrived)
    high_heads = return_heads(high_mixed)
    *low_heads, _ = lax.optimization_barrier((*low_heads, high_mixed[0]))

    def output_rows(chunk, heads, after):
        cut = [lax.dynamic_slice_in_dim(head, (1 - mine) * rows, rows, axis=0) for head in heads]
        heads = heads + [to_mod(jnp.stack(cut))]
        send_x, send_y, keep_a, keep_b = finish(chunk, meta, modality, after, heads, own_out, other_out)
        got_x, got_y = to_x(send_x), to_y(send_y)
        return got_x, got_y, keep_a, keep_b

    def added(got_x, got_y, keep_a, keep_b):
        got_x, got_y, keep_a, keep_b = [part.astype(jnp.float32) for part in (got_x, got_y, keep_a, keep_b)]
        last_a = to_y((keep_a[1] + got_x[1]).astype(jnp.bfloat16)).astype(jnp.float32)
        last_b = to_x((keep_b[1] + got_y[1]).astype(jnp.bfloat16)).astype(jnp.float32)
        result = jnp.concatenate([keep_a[0] + got_x[0] + last_a, keep_b[0] + got_y[0] + last_b])
        return result.astype(jnp.bfloat16)

    low_rows = output_rows(0, low_heads, high_heads[1])
    high_rows = output_rows(1, high_heads, low_rows[2])
    results = [added(*low_rows), added(*high_rows)]
    back = to_mod(jnp.where(first, results[1], results[0]))
    return jnp.concatenate(
        [jnp.where(first, results[0], back), jnp.where(first, back, results[1])], axis=0
    )


def solution(mesh):
    sizes = dict(mesh.shape)
    in_specs = (
        P(("mod", "seq"), "tp"),
        P(),
        P(),
        P("mod", None, None, "tp"),
        P(),
        P("mod", "tp", None),
    )
    out_specs = P(("mod", "seq"), "tp")

    def run(tokens, modality, norm_gain, input_weight, head_gain, output_weight):
        heads = input_weight.shape[3] // HD
        shard = tokens.shape[0] // (sizes["mod"] * sizes["seq"])
        small = (sizes["mod"], sizes["seq"], sizes["tp"]) == (2, 4, 4)
        fits = small and heads == 32 and shard == 8 * SPAN
        return jax.shard_map(
            body if fits else general_body,
            mesh=mesh,
            in_specs=in_specs,
            out_specs=out_specs,
            check_vma=False,
        )(tokens, modality, norm_gain, input_weight, head_gain, output_weight)

    return run
```
